256 devices in a mesh: dom: 32 (over y, z), feat: 8 (over x, core).
Axes of the slice: x: 4, y: 4, z: 8, core: 2. Of those that a mesh axis runs over, the one named last changes fastest.
Arguments:
- node_feats: bfloat16 [262144, 128], P(('dom', 'feat')), may hold values from -6 to 6
- cached_feats: bfloat16 [131072, 128], P(('dom', 'feat')), may hold values from -6 to 6
- tile_values: bfloat16 [65536, 128, 128], P(('dom', 'feat')), may hold values from -0.125 to 0.125
- tile_row: int32 [256, 256], P(('dom', 'feat')), may hold values from 0 to 7
- tile_col: int32 [256, 256], P(('dom', 'feat')), may hold values from 0 to 75
- tile_count: int32 [256], P(('dom', 'feat')), may hold values from 1 to 256, as said below
- need_blocks: int32 [256, 32, 2], P(('dom', 'feat')), may hold values from 0 to 11
- weights: bfloat16 [128, 128], replicated, may hold values from -0.5 to 0.5
- grad_out: bfloat16 [262144, 128], P(('dom', 'feat')), may hold values from -6 to 6
Outputs:
- output: bfloat16 [262144, 128], P(('dom', 'feat'))
- h_grad: bfloat16 [262144, 128], P(('dom', 'feat'))
- w_grad: float32 [128, 128], replicated
The draws below stay inside these ranges and needn't reach their ends.
Inputs may be any that keep to these rules, and one draw needn't show every extreme that they name: `tile_count`: slots at or beyond a device's count are unused; some device uses all 256 slots. `tile_row`: local row block of each slot. `tile_col`: below 12: one of the device's own source blocks; else 12 + p * 2 + s names slot s of the blocks taken from partition p of the same batch. need_blocks[g, p, s] is a source block of partition p of device g's batch.
All inputs are finite; a program needn't handle non-finite values.
Results may differ from the reference program's by a relative error of at most 0.0061.
Values may be sent and summed in bfloat16 or wider, within the bound.
A program may use at most 128 MiB of HBM per device.

```python
import math
import jax
import jax.numpy as jnp
from jax import lax

F_IN = 128
HID = 128
TB = 128
BLK_DEV = 8
HIST_DEV = 4
SLOT = 2
TILE_CAP = 256
PEERS = 32
SRC_DEV = 12
NCOL = 76
NODES = 262144
HROWS = 131072
N_DOM = 32
N_FEAT = 8
DEVICES = 256


def draw_tile_count(key, part):
    key = jax.random.fold_in(key, 7)
    first, second = jax.random.split(key)
    lowest = max(1, TILE_CAP // 8)
    counts = jax.random.randint(first, (DEVICES,), lowest, TILE_CAP * 3 // 4 + 1)
    busiest = jax.random.randint(second, (), 0, DEVICES)
    return jnp.where(jnp.arange(DEVICES, dtype=jnp.int32) == busiest, TILE_CAP, counts).astype(jnp.int32)


def with_ends(array, own_key, smallest, top_value):
    shape = array.shape
    index_at = [jax.random.randint(jax.random.fold_in(own_key, axis), (), 0, shape[axis]) for axis in range(len(shape))]
    array = array.at[tuple(index_at)].set(smallest)
    longest = shape.index(max(shape))
    index_at[longest] = (index_at[longest] + 1) % shape[longest]
    return array.at[tuple(index_at)].set(top_value)


def levels(stream_key, extent, shards, smallest, largest):
    def one(position, parts):
        steps = jax.random.uniform(jax.random.fold_in(jax.random.fold_in(stream_key, 6), position), (parts,), jnp.float32, smallest / len(shards), largest / len(shards))
        return jnp.repeat(jnp.exp(steps), extent[position] // parts).reshape((-1,) + (1,) * (len(extent) - position - 1))

    gain = one(*shards[0])
    for cut in shards[1:]:
        gain = gain * one(*cut)
    return gain


def normal_values(rng, shape, width, limit, cuts=(), kind=jnp.bfloat16):
    array = jax.random.normal(rng, shape, jnp.float32) * width
    if len(cuts) > 0:
        array = levels(rng, shape, cuts, -0.22, 0.18) * array
    return jnp.clip(array, min=-limit, max=limit).astype(kind)


def setup_inputs(seed: int = 0) -> dict:
    seeds = jax.random.split(jax.random.key(seed), 10)
    return {
        "node_feats": normal_values(seeds[0], (NODES, F_IN), 1.0, 6.0, ((0, 256),)),
        "cached_feats": normal_values(seeds[1], (HROWS, F_IN), 1.0, 6.0, ((0, 256),)),
        "tile_values": normal_values(seeds[2], (DEVICES * TILE_CAP, TB, TB), (TB * TILE_CAP // (2 * BLK_DEV)) ** -0.5, 0.125, ((0, 256),)),
        "tile_row": with_ends(jax.random.randint(seeds[3], (DEVICES, TILE_CAP), 0, BLK_DEV), jax.random.fold_in(seeds[3], 1), 0, BLK_DEV - 1).astype(jnp.int32),
        "tile_col": with_ends(jax.random.randint(seeds[4], (DEVICES, TILE_CAP), 0, NCOL), jax.random.fold_in(seeds[4], 1), 0, NCOL - 1).astype(jnp.int32),
        "tile_count": draw_tile_count(jax.random.fold_in(seeds[9], 71), 0),
        "need_blocks": with_ends(jax.random.randint(seeds[6], (DEVICES, PEERS, SLOT), 0, SRC_DEV), jax.random.fold_in(seeds[6], 1), 0, SRC_DEV - 1).astype(jnp.int32),
        "weights": normal_values(seeds[7], (F_IN, HID), F_IN ** -0.5, 0.5),
        "grad_out": normal_values(seeds[8], (NODES, HID), 1.0, 6.0, ((0, 256),)),
    }


def reference(node_feats, cached_feats, tile_values, tile_row, tile_col, tile_count, need_blocks, weights, grad_out):
    device_count = N_DOM * N_FEAT
    sources = jnp.concatenate([node_feats.reshape(device_count, BLK_DEV, TB, F_IN), cached_feats.reshape(device_count, HIST_DEV, TB, F_IN)], axis=1)
    flat_sources = sources.reshape(device_count * SRC_DEV, TB, F_IN)
    device_ids = jnp.arange(device_count, dtype=jnp.int32)
    replica_id = device_ids % N_FEAT
    peer_device = jnp.arange(N_DOM, dtype=jnp.int32)[None, :] * N_FEAT + replica_id[:, None]
    slot_global = (peer_device[:, :, None] * SRC_DEV + need_blocks).reshape(device_count, N_DOM * SLOT).astype(jnp.int32)
    own_global = device_ids[:, None] * SRC_DEV + jnp.arange(SRC_DEV, dtype=jnp.int32)[None, :]
    column_map = jnp.concatenate([own_global, slot_global], axis=1)
    tile_global = jnp.take_along_axis(column_map, tile_col, axis=1)
    tile_sets = tile_values.reshape(device_count, TILE_CAP, TB, TB)
    active = (jnp.arange(TILE_CAP, dtype=jnp.int32)[None, :] < tile_count[:, None]).astype(jnp.float32)

    def gather_rows(packed):
        tile_set, global_ids, row_ids, mask = packed
        picked = flat_sources[global_ids].astype(jnp.float32)
        product = jnp.einsum('tij,tjf->tif', tile_set.astype(jnp.float32), picked)
        return jnp.zeros((BLK_DEV, TB, F_IN), jnp.float32).at[row_ids].add(product * mask[:, None, None])
    mixed = lax.map(gather_rows, (tile_sets, tile_global, tile_row, active))
    mixed = mixed.astype(jnp.bfloat16).reshape(NODES, F_IN)
    pre_act = jnp.dot(mixed, weights, preferred_element_type=jnp.float32)
    sig = jax.nn.sigmoid(pre_act)
    output = (pre_act * sig).astype(jnp.bfloat16)
    act_grad = (grad_out.astype(jnp.float32) * sig * (1.0 + pre_act * (1.0 - sig))).astype(jnp.bfloat16)
    mixed_grad = jnp.dot(act_grad, weights.T, preferred_element_type=jnp.float32).astype(jnp.bfloat16)
    grad_blocks = mixed_grad.reshape(device_count, BLK_DEV, TB, F_IN)

    def spread_cols(total, packed):
        tile_set, global_ids, row_ids, mask, blocks_here = packed
        picked = blocks_here[row_ids].astype(jnp.float32)
        product = jnp.einsum('tij,tif->tjf', tile_set.astype(jnp.float32), picked)
        return (total.at[global_ids].add(product * mask[:, None, None]), None)
    start = jnp.zeros((device_count * SRC_DEV, TB, F_IN), jnp.float32)
    summed, unused = lax.scan(spread_cols, start, (tile_sets, tile_global, tile_row, active, grad_blocks))
    h_grad = summed.reshape(device_count, SRC_DEV, TB, F_IN)[:, :BLK_DEV].reshape(NODES, F_IN).astype(jnp.bfloat16)
    w_grad = jnp.dot(mixed.T, act_grad, preferred_element_type=jnp.float32) * (1.0 / math.sqrt(NODES))
    return (output, h_grad, w_grad)
```

```python
import functools
import math

import jax
import jax.numpy as jnp
from jax import lax
from jax.experimental import pallas as pl
from jax.experimental.pallas import tpu as pltpu
from jax.sharding import PartitionSpec as P

MESH = pl.DeviceIdType.MESH
VMEM = pltpu.VMEM
SMEM = pltpu.SMEM
DMA = pltpu.SemaphoreType.DMA
NY = 4
NZ = 8
TB = 128
SRC = 12
BLK = 8
SLOT = 2
NSLOT = NY * NZ * SLOT
NF = 8
W_SCALE = 1.0 / math.sqrt(BLK * TB * NY * NZ * NF)
UNROLL = 8


def _place():
    me = lax.axis_index("dom")
    return me // NZ, lax.rem(me, NZ)


def _at(y, z):
    return {"dom": lax.rem(y + NY, NY) * NZ + lax.rem(z + NZ, NZ)}


def _barrier(peers):
    sem = pltpu.get_barrier_semaphore()
    for peer in peers:
        pl.semaphore_signal(sem, inc=1, device_id=peer, device_id_type=MESH)
    pl.semaphore_wait(sem, len(peers))


GATHER_ORDER = (0, -1, 1, -2, 2, -3, 3, 4)


def gather_kernel(
    node, cached, need_v, need_s, gathered, peer_need,
    own, zp0, zm0, zp1, zm1, zp2, zm2, zfar, stage, pn_v, pn_s,
    in_sem, need_send, need_recv, pn_sem, z_send, z_recv, y_send, y_recv, keep_sem,
):
    y, z = _place()
    loads = [
        pltpu.make_async_copy(node, own.at[pl.ds(0, BLK)], in_sem.at[0]),
        pltpu.make_async_copy(cached, own.at[pl.ds(BLK, SRC - BLK)], in_sem.at[1]),
    ]
    for copy in loads:
        copy.start()
    _barrier([_at(y, z + 1), _at(y, z - 1)] + [_at(y + dy, z) for dy in range(1, NY)])
    asks = [
        pltpu.make_async_remote_copy(
            src_ref=need_v, dst_ref=pn_v.at[dy - 1],
            send_sem=need_send.at[dy - 1], recv_sem=need_recv.at[dy - 1],
            device_id=_at(y + dy, z), device_id_type=MESH,
        )
        for dy in range(1, NY)
    ]
    for copy in asks:
        copy.start()
    for copy in loads:
        copy.wait()
    half = SRC // 2
    first, second = pl.ds(0, half), pl.ds(half, half)

    def hop(src, dst, slot, dz):
        return pltpu.make_async_remote_copy(
            src_ref=src, dst_ref=dst, send_sem=z_send.at[slot], recv_sem=z_recv.at[slot],
            device_id=_at(y, z + dz), device_id_type=MESH,
        )

    def chain(stops, slot, dz, last):
        pairs = []
        for i in range(3):
            pairs.append(
                [
                    hop(stops[i].at[part], stops[i + 1].at[part], slot + 2 * i + n, dz)
                    for n, part in enumerate((first, second))
                ]
            )
        pairs.append([hop(stops[3].at[last], zfar.at[last], slot + 6, dz)])
        return pairs

    up = chain((own, zp0, zp1, zp2), 0, 1, first)
    down = chain((own, zm0, zm1, zm2), 7, -1, second)
    for n in range(2):
        up[0][n].start()
        down[0][n].start()
    for copy in asks:
        copy.wait()
    to_scalar = pltpu.make_async_copy(pn_v, pn_s, pn_sem)
    to_scalar.start()
    peer_need[...] = pn_v[...]
    to_scalar.wait()

    sends = []
    keeps = []

    def serve(buf, k):
        z0 = lax.rem(z + GATHER_ORDER[k] + NZ, NZ)
        mine = (y * NZ + z0) * SLOT
        for dy in range(1, NY):
            for s in range(SLOT):
                stage[dy, k, s] = buf[pn_s[NY - 1 - dy, 0, y * NZ + z0, s]]
            copy = pltpu.make_async_remote_copy(
                src_ref=stage.at[dy, k], dst_ref=gathered.at[pl.ds(mine, SLOT)],
                send_sem=y_send.at[dy - 1, k], recv_sem=y_recv.at[dy - 1, k],
                device_id=_at(y + dy, z), device_id_type=MESH,
            )
            copy.start()
            sends.append((dy, k, copy))
        for s in range(SLOT):
            stage[0, k, s] = buf[need_s[0, y * NZ + z0, s]]
        copy = pltpu.make_async_copy(
            stage.at[0, k], gathered.at[pl.ds(mine, SLOT)], keep_sem.at[k]
        )
        copy.start()
        keeps.append(copy)

    serve(own, 0)
    for step, (a, b) in enumerate(((zp0, zm0), (zp1, zm1), (zp2, zm2))):
        for n in range(2):
            for chained, forward in ((up, 0), (down, 1)):
                chained[step][n].wait_recv()
                if step < 2:
                    chained[step + 1][n].start()
                elif n == forward:
                    chained[3][0].start()
        serve(a, 1 + 2 * step)
        serve(b, 2 + 2 * step)
    up[3][0].wait_recv()
    down[3][0].wait_recv()
    serve(zfar, 7)
    for pairs in up + down:
        for copy in pairs:
            copy.wait_send()
    for copy in keeps:
        copy.wait()
    for dy, k, copy in sends:
        copy.wait_send()
        z0 = lax.rem(z + GATHER_ORDER[k] + NZ, NZ)
        theirs = (lax.rem(y + NY - dy, NY) * NZ + z0) * SLOT
        pltpu.make_async_remote_copy(
            src_ref=stage.at[dy, k], dst_ref=gathered.at[pl.ds(theirs, SLOT)],
            send_sem=y_send.at[dy - 1, k], recv_sem=y_recv.at[dy - 1, k],
            device_id=_at(y - dy, z), device_id_type=MESH,
        ).wait_recv()


def gather(node, cached, need):
    block = (SRC, TB, TB)
    return pl.pallas_call(
        gather_kernel,
        out_shape=(
            jax.ShapeDtypeStruct((NSLOT, TB, TB), jnp.bfloat16),
            jax.ShapeDtypeStruct((NY - 1, 1, NY * NZ, SLOT), jnp.int32),
        ),
        in_specs=[
            pl.BlockSpec(memory_space=pl.ANY),
            pl.BlockSpec(memory_space=pl.ANY),
            pl.BlockSpec(memory_space=VMEM),
            pl.BlockSpec(memory_space=SMEM),
        ],
        out_specs=(pl.BlockSpec(memory_space=pl.ANY), pl.BlockSpec(memory_space=VMEM)),
        scratch_shapes=[VMEM(block, jnp.bfloat16) for _ in range(8)]
        + [
            VMEM((NY, NZ, SLOT, TB, TB), jnp.bfloat16),
            VMEM((NY - 1, 1, NY * NZ, SLOT), jnp.int32),
            SMEM((NY - 1, 1, NY * NZ, SLOT), jnp.int32),
            DMA((2,)),
            DMA((NY - 1,)),
            DMA((NY - 1,)),
            DMA,
            DMA((14,)),
            DMA((14,)),
            DMA((NY - 1, NZ)),
            DMA((NY - 1, NZ)),
            DMA((NZ,)),
        ],
        compiler_params=pltpu.CompilerParams(
            collective_id=0, has_side_effects=True, vmem_limit_bytes=60 * 2**20
        ),
    )(node, cached, need, need)


def layer_kernel(
    row, col, count, tiles_h, node, cached, gathered, weights, grad_out,
    output, contrib, local_part, w_local,
    tiles, table, mixed_acc, grads_t, spread, tile_sem, table_sem,
):
    cap = tiles_h.shape[0]
    chunk = cap // 8
    table_loads = [
        pltpu.make_async_copy(node, table.at[pl.ds(0, BLK)], table_sem.at[0]),
        pltpu.make_async_copy(cached, table.at[pl.ds(BLK, SRC - BLK)], table_sem.at[1]),
        pltpu.make_async_copy(gathered, table.at[pl.ds(SRC, NSLOT)], table_sem.at[2]),
    ]
    for copy in table_loads:
        copy.start()

    def tile_load(i):
        span = pl.ds(i * chunk, chunk)
        return pltpu.make_async_copy(tiles_h.at[span], tiles.at[span], tile_sem.at[i])

    for i in range(8):
        tile_load(i).start()
    zero_src = SRC + NSLOT
    table[zero_src] = jnp.zeros((TB, TB), jnp.bfloat16)
    mixed_acc[...] = jnp.zeros_like(mixed_acc)
    used = count[0]
    for copy in table_loads:
        copy.wait()

    def steps(i):
        return jnp.clip((used - i * chunk + UNROLL - 1) // UNROLL, 0, chunk // UNROLL)

    def forward_chunk(i, _):
        tile_load(i).wait()

        def step(j, _):
            base = i * chunk + j * UNROLL
            products = []
            for u in range(UNROLL):
                t = base + u
                c = jnp.where(t < used, col[0, t], zero_src)
                products.append(jnp.dot(tiles[t], table[c], preferred_element_type=jnp.float32))
            for u in range(UNROLL):
                r = row[0, base + u]
                mixed_acc[r] += products[u]
            return 0

        return lax.fori_loop(0, steps(i), step, 0)

    lax.fori_loop(0, 8, forward_chunk, 0)

    w = weights[...]
    w_sum = jnp.zeros((TB, TB), jnp.float32)
    for r in range(BLK):
        mixed = mixed_acc[r].astype(jnp.bfloat16)
        pre = jnp.dot(mixed, w, preferred_element_type=jnp.float32)
        sig = jax.nn.sigmoid(pre)
        output[r] = (pre * sig).astype(jnp.bfloat16)
        act = (grad_out[r].astype(jnp.float32) * sig * (1.0 + pre * (1.0 - sig))).astype(jnp.bfloat16)
        grads_t[r] = lax.dot_general(
            w, act, (((1,), (1,)), ((), ())), preferred_element_type=jnp.float32
        ).astype(jnp.bfloat16)
        w_sum += lax.dot_general(
            mixed, act, (((0,), (0,)), ((), ())), preferred_element_type=jnp.float32
        )
    w_local[...] = w_sum
    grads_t[BLK] = jnp.zeros((TB, TB), jnp.bfloat16)
    spread[...] = jnp.zeros_like(spread)

    def backward_step(j, _):
        base = j * UNROLL
        products = []
        for u in range(UNROLL):
            t = base + u
            r = jnp.where(t < used, row[0, t], BLK)
            products.append(jnp.dot(grads_t[r], tiles[t], preferred_element_type=jnp.float32))
        for u in range(UNROLL):
            c = col[0, base + u]
            spread[c] += products[u]
        return 0

    lax.fori_loop(0, (used + UNROLL - 1) // UNROLL, backward_step, 0)
    for b in range(BLK):
        local_part[b] = spread[b]

    def cast(s, _):
        contrib[s] = spread[SRC + s].astype(jnp.bfloat16)
        return 0

    lax.fori_loop(0, NSLOT, cast, 0)


def layer(row, col, count, tiles, node, cached, gathered, weights, grad_out):
    cap = tiles.shape[0]
    flops = 4 * cap * TB**3
    vmem = pl.BlockSpec(memory_space=VMEM)
    smem = pl.BlockSpec(memory_space=SMEM)
    hbm = pl.BlockSpec(memory_space=pl.ANY)
    return pl.pallas_call(
        layer_kernel,
        out_shape=(
            jax.ShapeDtypeStruct((BLK, TB, TB), jnp.bfloat16),
            jax.ShapeDtypeStruct((NSLOT, TB, TB), jnp.bfloat16),
            jax.ShapeDtypeStruct((BLK, TB, TB), jnp.float32),
            jax.ShapeDtypeStruct((TB, TB), jnp.float32),
        ),
        in_specs=[smem, smem, smem, hbm, hbm, hbm, hbm, vmem, vmem],
        out_specs=(vmem, vmem, vmem, vmem),
        scratch_shapes=[
            VMEM((cap, TB, TB), jnp.bfloat16),
            VMEM((SRC + NSLOT + 1, TB, TB), jnp.bfloat16),
            VMEM((BLK, TB, TB), jnp.float32),
            VMEM((BLK + 1, TB, TB), jnp.bfloat16),
            VMEM((SRC + NSLOT, TB, TB), jnp.float32),
            DMA((8,)),
            DMA((3,)),
        ],
        compiler_params=pltpu.CompilerParams(vmem_limit_bytes=60 * 2**20),
        cost_estimate=pl.CostEstimate(
            flops=flops, bytes_accessed=16 * 2**20, transcendentals=BLK * TB * TB
        ),
    )(row, col, count, tiles, node, cached, gathered, weights, grad_out)


SCATTER_ORDER = (4, 3, -3, 2, -2, 1, -1, 0)


def scatter_kernel(
    contrib, local_part, w_local, need_s, peer_need, h_grad, w_grad,
    ybuf, ownc, sp4, sm4, sp3, sm3, sp2, sm2, sp1, sm1,
    rp3, rm3, rp2, rm2, rp1, rm1, rp0, rm0, h_sum,
    wf, wy, wz, own_sem, y_send, y_recv, z_send, z_recv,
    wf_send, wf_recv, wy_send, wy_recv, wz_send, wz_recv, wg_send, wg_recv,
):
    y, z = _place()
    f = lax.axis_index("feat")
    mine = pltpu.make_async_copy(contrib.at[pl.ds(y * NZ * SLOT, NZ * SLOT)], ownc, own_sem)
    mine.start()
    peers_f = [{"feat": lax.rem(f + df, NF)} for df in range(1, NF)]
    peers_y = [_at(y + dy, z) for dy in range(1, NY)]
    peers_z = [_at(y, z + dz) for dz in range(1, NZ)]
    _barrier(peers_f + peers_y + peers_z)
    piece = TB // NF

    def rows_of(i):
        return pl.ds(pl.multiple_of(i * piece, piece), piece)

    def tell(peers, srcs, dst, send_sem, recv_sem):
        copies = [
            pltpu.make_async_remote_copy(
                src_ref=src, dst_ref=dst, send_sem=send_sem.at[i], recv_sem=recv_sem.at[i],
                device_id=peer, device_id_type=MESH,
            )
            for i, (peer, src) in enumerate(zip(peers, srcs))
        ]
        for copy in copies:
            copy.start()
        return copies

    def finish(copies):
        for copy in copies:
            copy.wait()

    def summed(ref, n):
        acc = ref[0]
        for i in range(1, n):
            acc = acc + ref[i]
        return acc

    wf[f] = w_local[rows_of(f)]
    over_f = tell(
        peers_f, [w_local.at[rows_of(p["feat"])] for p in peers_f], wf.at[f], wf_send, wf_recv
    )
    sends = {}
    for k in range(NZ):
        z0 = lax.rem(z + SCATTER_ORDER[k] + NZ, NZ)
        for dy in range(1, NY):
            theirs = (lax.rem(y + dy, NY) * NZ + z0) * SLOT
            copy = pltpu.make_async_remote_copy(
                src_ref=contrib.at[pl.ds(theirs, SLOT)], dst_ref=ybuf.at[dy - 1, k],
                send_sem=y_send.at[dy - 1, k], recv_sem=y_recv.at[dy - 1, k],
                device_id=_at(y + dy, z), device_id_type=MESH,
            )
            copy.start()
            sends[dy, k] = copy
    mine.wait()
    half = BLK // 2
    rows = 32

    def total(k, lo, n, arrived, put):
        z0 = lax.rem(z + SCATTER_ORDER[k] + NZ, NZ)
        ids = [need_s[0, y * NZ + z0, s] for s in range(SLOT)]
        for dy in range(1, NY):
            ids += [peer_need[dy - 1, 0, y * NZ + z0, s] for s in range(SLOT)]

        def part(i, _):
            span = pl.ds(pl.multiple_of(i * rows, rows), rows)
            parts = [ownc[z0 * SLOT + s, span] for s in range(SLOT)]
            for dy in range(1, NY):
                parts += [ybuf[dy - 1, k, s, span] for s in range(SLOT)]
            parts = [p.astype(jnp.float32) for p in parts]
            for b in range(lo, lo + n):
                acc = arrived(b, span)
                for p, which in zip(parts, ids):
                    acc = acc + jnp.where(which == b, p, 0.0)
                put(b, span, acc)
            return 0

        lax.fori_loop(0, TB // rows, part, 0)

    def hop(src, dst, slot, dz):
        return pltpu.make_async_remote_copy(
            src_ref=src, dst_ref=dst, send_sem=z_send.at[slot], recv_sem=z_recv.at[slot],
            device_id=_at(y, z + dz), device_id_type=MESH,
        )

    def nothing(b, span):
        return jnp.zeros((rows, TB), jnp.float32)

    def into(ref, lo=0):
        def put(b, span, acc):
            ref[b - lo, span] = acc.astype(jnp.bfloat16)

        return put

    def arrive(k):
        for dy in range(1, NY):
            sends[dy, k].wait_recv()

    hops = []
    arrive(0)
    total(0, 0, half, nothing, into(sp4))
    hops.append(hop(sp4, rp3, 0, 1))
    hops[-1].start()
    total(0, half, half, nothing, into(sm4, half))
    hops.append(hop(sm4, rm3, 1, -1))
    hops[-1].start()

    def tail(ref, lo):
        def arrived(b, span):
            if lo <= b < lo + half:
                return ref[b - lo, span].astype(jnp.float32)
            return nothing(b, span)

        return arrived

    def whole(ref):
        return lambda b, span: ref[b, span].astype(jnp.float32)

    plan = (
        (rp3, sp3, rp2, 1), (rm3, sm3, rm2, -1),
        (rp2, sp2, rp1, 1), (rm2, sm2, rm1, -1),
        (rp1, sp1, rp0, 1), (rm1, sm1, rm0, -1),
    )
    for i, (got, out, there, dz) in enumerate(plan):
        k = i + 1
        if i == 1:
            finish(over_f)
            wy[y] = summed(wf, NF)
            over_y = tell(peers_y, [wy.at[y]] * (NY - 1), wy.at[y], wy_send, wy_recv)
        if i == 3:
            finish(over_y)
            wz[z] = summed(wy, NY)
            over_z = tell(peers_z, [wz.at[z]] * (NZ - 1), wz.at[z], wz_send, wz_recv)
        if i == 5:
            finish(over_z)
            w_grad[rows_of(f)] = summed(wz, NZ) * W_SCALE
            back = tell(
                peers_f, [w_grad.at[rows_of(f)]] * (NF - 1), w_grad.at[rows_of(f)], wg_send, wg_recv
            )
        arrive(k)
        hops[i].wait_recv()
        if i < 2:
            arrived = tail(got, 0 if dz == 1 else half)
        else:
            arrived = whole(got)
        total(k, 0, BLK, arrived, into(out))
        hops.append(hop(out, there, i + 2, dz))
        hops[-1].start()
    arrive(7)

    hops[6].wait_recv()
    hops[7].wait_recv()

    def last(b, span):
        return (
            local_part[b, span]
            + rp0[b, span].astype(jnp.float32)
            + rm0[b, span].astype(jnp.float32)
        )

    def put_last(b, span, acc):
        h_sum[b, span] = acc

    total(7, 0, BLK, last, put_last)
    for b in range(BLK):
        h_grad[b] = h_sum[b].T.astype(jnp.bfloat16)
    finish(back)
    for copy in hops:
        copy.wait_send()
    for copy in sends.values():
        copy.wait_send()


def scatter(contrib, local_part, w_local, need, peer_need):
    vmem = pl.BlockSpec(memory_space=VMEM)
    smem = pl.BlockSpec(memory_space=SMEM)
    bf = jnp.bfloat16
    blocks = [BLK // 2] * 2 + [BLK] * 6 + [BLK // 2] * 2 + [BLK] * 6
    return pl.pallas_call(
        scatter_kernel,
        out_shape=(
            jax.ShapeDtypeStruct((BLK, TB, TB), bf),
            jax.ShapeDtypeStruct((TB, TB), jnp.float32),
        ),
        in_specs=[pl.BlockSpec(memory_space=pl.ANY), vmem, vmem, smem, smem],
        out_specs=(vmem, vmem),
        scratch_shapes=[
            VMEM((NY - 1, NZ, SLOT, TB, TB), bf),
            VMEM((NZ * SLOT, TB, TB), bf),
        ]
        + [VMEM((n, TB, TB), bf) for n in blocks]
        + [VMEM((BLK, TB, TB), jnp.float32)]
        + [VMEM((n, TB // NF, TB), jnp.float32) for n in (NF, NY, NZ)]
        + [DMA, DMA((NY - 1, NZ)), DMA((NY - 1, NZ)), DMA((8,)), DMA((8,))]
        + [DMA((n - 1,)) for n in (NF, NF, NY, NY, NZ, NZ, NF, NF)],
        compiler_params=pltpu.CompilerParams(
            collective_id=1, has_side_effects=True, vmem_limit_bytes=60 * 2**20
        ),
    )(contrib, local_part, w_local, need, peer_need)


def body(node_feats, cached_feats, tile_values, tile_row, tile_col, tile_count, need_blocks, weights, grad_out):
    node = node_feats.reshape(BLK, TB, TB)
    cached = cached_feats.reshape(SRC - BLK, TB, TB)
    gathered, peer_need = gather(node, cached, need_blocks)
    output, contrib, local_part, w_local = layer(
        tile_row, tile_col, tile_count, tile_values, node, cached, gathered, weights,
        grad_out.reshape(BLK, TB, TB),
    )
    h_grad, w_grad = scatter(contrib, local_part, w_local, need_blocks, peer_need)
    return output.reshape(BLK * TB, TB), h_grad.reshape(BLK * TB, TB), w_grad


def solution(mesh):
    rows = P(("dom", "feat"), None)
    cubes = P(("dom", "feat"), None, None)
    in_specs = (rows, rows, cubes, rows, rows, P(("dom", "feat")), cubes, P(), rows)
    out_specs = (rows, rows, P())
    return jax.shard_map(body, mesh=mesh, in_specs=in_specs, out_specs=out_specs, check_vma=False)
```

```python
import functools
import math

import jax
import jax.numpy as jnp
from jax import lax
from jax.experimental import pallas as pl
from jax.experimental.pallas import tpu as pltpu
from jax.sharding import PartitionSpec as P

MESH = pl.DeviceIdType.MESH
VMEM = pltpu.VMEM
SMEM = pltpu.SMEM
DMA = pltpu.SemaphoreType.DMA
NY = 4
NZ = 8
TB = 128
SRC = 12
BLK = 8
SLOT = 2
NSLOT = NY * NZ * SLOT
NF = 8
W_SCALE = 1.0 / math.sqrt(BLK * TB * NY * NZ * NF)
GROUP = 32
CAST = 8


def _place():
    me = lax.axis_index("dom")
    return me // NZ, lax.rem(me, NZ)


def _at(y, z):
    return {"dom": lax.rem(y + NY, NY) * NZ + lax.rem(z + NZ, NZ)}


def _barrier(loads, peers):
    sem = pltpu.get_barrier_semaphore()
    for peer in peers:
        pl.semaphore_signal(sem, inc=1, device_id=peer, device_id_type=MESH)
    for copy in loads:
        copy.start()
    pl.semaphore_wait(sem, len(peers))


GATHER_ORDER = (0, -1, 1, -2, 2, -3, 3, 4)


def gather_kernel(
    node, cached, need, gathered, peer_need,
    own, need_s, zp0, zm0, zp1, zm1, zp2, zm2, zfar, stage, pn_v, pn_s,
    in_sem, need_send, need_recv, pn_sem, out_sem, z_send, z_recv, y_send, y_recv, keep_sem,
):
    y, z = _place()
    loads = [
        pltpu.make_async_copy(node, own.at[pl.ds(0, BLK)], in_sem.at[0]),
        pltpu.make_async_copy(cached, own.at[pl.ds(BLK, SRC - BLK)], in_sem.at[1]),
        pltpu.make_async_copy(need, need_s, in_sem.at[2]),
    ]
    _barrier(loads, [_at(y, z + 1), _at(y, z - 1)] + [_at(y + dy, z) for dy in range(1, NY)])
    asks = [
        pltpu.make_async_remote_copy(
            src_ref=need, dst_ref=pn_v.at[dy - 1],
            send_sem=need_send.at[dy - 1], recv_sem=need_recv.at[dy - 1],
            device_id=_at(y + dy, z), device_id_type=MESH,
        )
        for dy in range(1, NY)
    ]
    for copy in asks:
        copy.start()
    for copy in loads:
        copy.wait()
    half = SRC // 2
    first, second = pl.ds(0, half), pl.ds(half, half)

    def hop(src, dst, slot, dz):
        return pltpu.make_async_remote_copy(
            src_ref=src, dst_ref=dst, send_sem=z_send.at[slot], recv_sem=z_recv.at[slot],
            device_id=_at(y, z + dz), device_id_type=MESH,
        )

    def chain(stops, slot, dz, last):
        pairs = []
        for i in range(3):
            pairs.append(
                [
                    hop(stops[i].at[part], stops[i + 1].at[part], slot + 2 * i + n, dz)
                    for n, part in enumerate((first, second))
                ]
            )
        pairs.append([hop(stops[3].at[last], zfar.at[last], slot + 6, dz)])
        return pairs

    up = chain((own, zp0, zp1, zp2), 0, 1, first)
    down = chain((own, zm0, zm1, zm2), 7, -1, second)
    for n in range(2):
        up[0][n].start()
        down[0][n].start()
    for copy in asks:
        copy.wait()
    to_scalar = pltpu.make_async_copy(pn_v, pn_s, pn_sem)
    to_scalar.start()
    to_output = pltpu.make_async_copy(pn_v, peer_need, out_sem)
    to_output.start()
    to_scalar.wait()

    sends = []
    keeps = []

    def serve(buf, k):
        z0 = lax.rem(z + GATHER_ORDER[k] + NZ, NZ)
        mine = (y * NZ + z0) * SLOT
        for dy in range(1, NY):
            for s in range(SLOT):
                stage[dy, k, s] = buf[pn_s[NY - 1 - dy, 0, s, y * NZ + z0]]
            copy = pltpu.make_async_remote_copy(
                src_ref=stage.at[dy, k], dst_ref=gathered.at[pl.ds(mine, SLOT)],
                send_sem=y_send.at[dy - 1, k], recv_sem=y_recv.at[dy - 1, k],
                device_id=_at(y + dy, z), device_id_type=MESH,
            )
            copy.start()
            sends.append((dy, k, copy))
        for s in range(SLOT):
            stage[0, k, s] = buf[need_s[0, s, y * NZ + z0]]
        copy = pltpu.make_async_copy(
            stage.at[0, k], gathered.at[pl.ds(mine, SLOT)], keep_sem.at[k]
        )
        copy.start()
        keeps.append(copy)

    serve(own, 0)
    for step, (a, b) in enumerate(((zp0, zm0), (zp1, zm1), (zp2, zm2))):
        for n in range(2):
            for chained, forward in ((up, 0), (down, 1)):
                chained[step][n].wait_recv()
                if step < 2:
                    chained[step + 1][n].start()
                elif n == forward:
                    chained[3][0].start()
        serve(a, 1 + 2 * step)
        serve(b, 2 + 2 * step)
    up[3][0].wait_recv()
    down[3][0].wait_recv()
    serve(zfar, 7)
    for pairs in up + down:
        for copy in pairs:
            copy.wait_send()
    to_output.wait()
    for copy in keeps:
        copy.wait()
    for dy, k, copy in sends:
        copy.wait_send()
        z0 = lax.rem(z + GATHER_ORDER[k] + NZ, NZ)
        theirs = (lax.rem(y + NY - dy, NY) * NZ + z0) * SLOT
        pltpu.make_async_remote_copy(
            src_ref=stage.at[dy, k], dst_ref=gathered.at[pl.ds(theirs, SLOT)],
            send_sem=y_send.at[dy - 1, k], recv_sem=y_recv.at[dy - 1, k],
            device_id=_at(y - dy, z), device_id_type=MESH,
        ).wait_recv()


def gather(node, cached, need):
    block = (SRC, TB, TB)
    return pl.pallas_call(
        gather_kernel,
        out_shape=(
            jax.ShapeDtypeStruct((NSLOT, TB, TB), jnp.bfloat16),
            jax.ShapeDtypeStruct((NY - 1, 1, SLOT, NY * NZ), jnp.int32),
        ),
        in_specs=[pl.BlockSpec(memory_space=pl.ANY)] * 3,
        out_specs=(pl.BlockSpec(memory_space=pl.ANY),) * 2,
        scratch_shapes=[VMEM(block, jnp.bfloat16), SMEM((1, SLOT, NY * NZ), jnp.int32)]
        + [VMEM(block, jnp.bfloat16) for _ in range(7)]
        + [
            VMEM((NY, NZ, SLOT, TB, TB), jnp.bfloat16),
            VMEM((NY - 1, 1, SLOT, NY * NZ), jnp.int32),
            SMEM((NY - 1, 1, SLOT, NY * NZ), jnp.int32),
            DMA((3,)),
            DMA((NY - 1,)),
            DMA((NY - 1,)),
            DMA,
            DMA,
            DMA((14,)),
            DMA((14,)),
            DMA((NY - 1, NZ)),
            DMA((NY - 1, NZ)),
            DMA((NZ,)),
        ],
        compiler_params=pltpu.CompilerParams(
            collective_id=0, has_side_effects=True, vmem_limit_bytes=60 * 2**20
        ),
    )(node, cached, need)


def layer_kernel(
    row_h, col_h, count_h, tiles_h, node, cached, gathered, weights_h, grad_out_h,
    output_h, contrib_h, local_h, w_local_h,
    row, col, count, weights, grad_out, output, contrib, w_local,
    tiles, table, mixed_acc, grads_t, spread, tile_sem, in_sem, out_sem, spread_sem,
):
    index_loads = [
        pltpu.make_async_copy(src, dst, in_sem.at[i])
        for i, (src, dst) in enumerate(((count_h, count), (row_h, row), (col_h, col)))
    ]
    table_loads = [
        pltpu.make_async_copy(gathered, table.at[pl.ds(SRC, NSLOT)], in_sem.at[3]),
        pltpu.make_async_copy(node, table.at[pl.ds(0, BLK)], in_sem.at[4]),
        pltpu.make_async_copy(cached, table.at[pl.ds(BLK, SRC - BLK)], in_sem.at[5]),
    ]
    dense_loads = [
        pltpu.make_async_copy(weights_h, weights, in_sem.at[6]),
        pltpu.make_async_copy(grad_out_h, grad_out, in_sem.at[7]),
    ]
    for copy in index_loads + table_loads:
        copy.start()

    def tile_load(i):
        span = pl.ds(i * GROUP, GROUP)
        return pltpu.make_async_copy(tiles_h.at[span], tiles.at[span], tile_sem.at[i])

    index_loads[0].wait()
    used = count[0]
    groups = (used + GROUP - 1) // GROUP

    def start_tiles(i, _):
        tile_load(i).start()
        return 0

    lax.fori_loop(0, groups, start_tiles, 0)
    for copy in dense_loads:
        copy.start()
    zero_src = SRC + NSLOT
    table[zero_src] = jnp.zeros((TB, TB), jnp.bfloat16)
    grads_t[BLK] = jnp.zeros((TB, TB), jnp.bfloat16)
    mixed_acc[...] = jnp.zeros_like(mixed_acc)

    def clear(c, _):
        spread[c] = jnp.zeros((TB, TB), jnp.float32)
        return 0

    lax.fori_loop(0, SRC + NSLOT, clear, 0)
    for copy in index_loads[1:] + table_loads:
        copy.wait()

    def forward_step(i, _):
        tile_load(i).wait()
        products = []
        for u in range(GROUP):
            t = i * GROUP + u
            c = jnp.where(t < used, col[0, t], zero_src)
            products.append(jnp.dot(tiles[t], table[c], preferred_element_type=jnp.float32))
        for u in range(GROUP):
            r = row[0, i * GROUP + u]
            mixed_acc[r] += products[u]
        return 0

    lax.fori_loop(0, groups, forward_step, 0)
    for copy in dense_loads:
        copy.wait()

    w = weights[...]
    w_sum = jnp.zeros((TB, TB), jnp.float32)
    for r in range(BLK):
        mixed = mixed_acc[r].astype(jnp.bfloat16)
        pre = jnp.dot(mixed, w, preferred_element_type=jnp.float32)
        sig = jax.nn.sigmoid(pre)
        output[r] = (pre * sig).astype(jnp.bfloat16)
        act = (grad_out[r].astype(jnp.float32) * sig * (1.0 + pre * (1.0 - sig))).astype(jnp.bfloat16)
        grads_t[r] = lax.dot_general(
            w, act, (((1,), (1,)), ((), ())), preferred_element_type=jnp.float32
        ).astype(jnp.bfloat16)
        w_sum += lax.dot_general(
            mixed, act, (((0,), (0,)), ((), ())), preferred_element_type=jnp.float32
        )
    w_local[...] = w_sum
    stores = [
        pltpu.make_async_copy(output, output_h, out_sem.at[0]),
        pltpu.make_async_copy(w_local, w_local_h, out_sem.at[1]),
    ]
    for copy in stores:
        copy.start()

    def backward_step(i, _):
        products = []
        for u in range(GROUP):
            t = i * GROUP + u
            r = jnp.where(t < used, row[0, t], BLK)
            products.append(jnp.dot(grads_t[r], tiles[t], preferred_element_type=jnp.float32))
        for u in range(GROUP):
            c = col[0, i * GROUP + u]
            spread[c] += products[u]
        return 0

    lax.fori_loop(0, groups, backward_step, 0)
    stores.append(pltpu.make_async_copy(spread.at[pl.ds(0, BLK)], local_h, out_sem.at[2]))
    stores[-1].start()

    def store_part(i):
        span = pl.ds(i * CAST, CAST)
        return pltpu.make_async_copy(contrib.at[span], contrib_h.at[span], spread_sem.at[i])

    def cast(i, _):
        for u in range(CAST):
            s = i * CAST + u
            contrib[s] = spread[SRC + s].astype(jnp.bfloat16)
        store_part(i).start()
        return 0

    lax.fori_loop(0, NSLOT // CAST, cast, 0)
    for i in range(NSLOT // CAST):
        store_part(i).wait()
    for copy in stores:
        copy.wait()


def layer(row, col, count, tiles, node, cached, gathered, weights, grad_out):
    cap = tiles.shape[0]
    flops = 4 * cap * TB**3
    hbm = pl.BlockSpec(memory_space=pl.ANY)
    bf, f32 = jnp.bfloat16, jnp.float32
    return pl.pallas_call(
        layer_kernel,
        out_shape=(
            jax.ShapeDtypeStruct((BLK, TB, TB), bf),
            jax.ShapeDtypeStruct((NSLOT, TB, TB), bf),
            jax.ShapeDtypeStruct((BLK, TB, TB), f32),
            jax.ShapeDtypeStruct((TB, TB), f32),
        ),
        in_specs=[hbm] * 9,
        out_specs=(hbm,) * 4,
        scratch_shapes=[
            SMEM((1, cap), jnp.int32),
            SMEM((1, cap), jnp.int32),
            SMEM((1,), jnp.int32),
            VMEM((TB, TB), bf),
            VMEM((BLK, TB, TB), bf),
            VMEM((BLK, TB, TB), bf),
            VMEM((NSLOT, TB, TB), bf),
            VMEM((TB, TB), f32),
            VMEM((cap, TB, TB), bf),
            VMEM((SRC + NSLOT + 1, TB, TB), bf),
            VMEM((BLK, TB, TB), f32),
            VMEM((BLK + 1, TB, TB), bf),
            VMEM((SRC + NSLOT, TB, TB), f32),
            DMA((cap // GROUP,)),
            DMA((8,)),
            DMA((3,)),
            DMA((NSLOT // CAST,)),
        ],
        compiler_params=pltpu.CompilerParams(vmem_limit_bytes=60 * 2**20),
        cost_estimate=pl.CostEstimate(
            flops=flops, bytes_accessed=16 * 2**20, transcendentals=BLK * TB * TB
        ),
    )(row, col, count, tiles, node, cached, gathered, weights, grad_out)


SCATTER_ORDER = (4, 3, -3, 2, -2, 1, -1, 0)


def scatter_kernel(
    contrib, local_h, w_local_h, need_h, peer_need_h, h_grad_h, w_grad_h,
    local_part, w_local, need_s, peer_need, h_grad, w_grad, ybuf, ownc, sp4, sm4, sp3, sm3, sp2, sm2, sp1, sm1,
    rp3, rm3, rp2, rm2, rp1, rm1, rp0, rm0, h_sum,
    wf, wy, wz, own_sem, y_send, y_recv, z_send, z_recv,
    load_sem, out_sem, wf_send, wf_recv, wy_send, wy_recv, wz_send, wz_recv, wg_send, wg_recv,
):
    y, z = _place()
    f = lax.axis_index("feat")
    mine = pltpu.make_async_copy(contrib.at[pl.ds(y * NZ * SLOT, NZ * SLOT)], ownc, own_sem)
    loads = [
        pltpu.make_async_copy(src, dst, load_sem.at[i])
        for i, (src, dst) in enumerate(
            (
                (w_local_h, w_local), (local_h, local_part),
                (need_h, need_s), (peer_need_h, peer_need),
            )
        )
    ]
    peers_f = [{"feat": lax.rem(f + df, NF)} for df in range(1, NF)]
    peers_y = [_at(y + dy, z) for dy in range(1, NY)]
    peers_z = [_at(y, z + dz) for dz in range(1, NZ)]
    _barrier([mine] + loads, peers_f + peers_y + peers_z)
    piece = TB // NF

    def rows_of(i):
        return pl.ds(pl.multiple_of(i * piece, piece), piece)

    def tell(peers, srcs, dst, send_sem, recv_sem):
        copies = [
            pltpu.make_async_remote_copy(
                src_ref=src, dst_ref=dst, send_sem=send_sem.at[i], recv_sem=recv_sem.at[i],
                device_id=peer, device_id_type=MESH,
            )
            for i, (peer, src) in enumerate(zip(peers, srcs))
        ]
        for copy in copies:
            copy.start()
        return copies

    def finish(copies):
        for copy in copies:
            copy.wait()

    def summed(ref, n):
        acc = ref[0]
        for i in range(1, n):
            acc = acc + ref[i]
        return acc

    loads[0].wait()
    wf[f] = w_local[rows_of(f)]
    over_f = tell(
        peers_f, [w_local.at[rows_of(p["feat"])] for p in peers_f], wf.at[f], wf_send, wf_recv
    )
    sends = {}

    def send(k):
        z0 = lax.rem(z + SCATTER_ORDER[k] + NZ, NZ)
        for dy in range(1, NY):
            theirs = (lax.rem(y + dy, NY) * NZ + z0) * SLOT
            copy = pltpu.make_async_remote_copy(
                src_ref=contrib.at[pl.ds(theirs, SLOT)], dst_ref=ybuf.at[dy - 1, k],
                send_sem=y_send.at[dy - 1, k], recv_sem=y_recv.at[dy - 1, k],
                device_id=_at(y + dy, z), device_id_type=MESH,
            )
            copy.start()
            sends[dy, k] = copy

    send(0)
    finish(over_f)
    wy[y] = summed(wf, NF)
    over_y = tell(peers_y, [wy.at[y]] * (NY - 1), wy.at[y], wy_send, wy_recv)
    send(1)
    send(2)
    for copy in [mine] + loads[1:]:
        copy.wait()
    half = BLK // 2
    rows = 32

    def total(k, lo, n, arrived, put):
        z0 = lax.rem(z + SCATTER_ORDER[k] + NZ, NZ)
        ids = [need_s[0, s, y * NZ + z0] for s in range(SLOT)]
        for dy in range(1, NY):
            ids += [peer_need[dy - 1, 0, s, y * NZ + z0] for s in range(SLOT)]

        def part(i, _):
            span = pl.ds(pl.multiple_of(i * rows, rows), rows)
            parts = [ownc[z0 * SLOT + s, span] for s in range(SLOT)]
            for dy in range(1, NY):
                parts += [ybuf[dy - 1, k, s, span] for s in range(SLOT)]
            parts = [p.astype(jnp.float32) for p in parts]
            for b in range(lo, lo + n):
                acc = arrived(b, span)
                for p, which in zip(parts, ids):
                    acc = acc + jnp.where(which == b, p, 0.0)
                put(b, span, acc)
            return 0

        lax.fori_loop(0, TB // rows, part, 0)

    def hop(src, dst, slot, dz):
        return pltpu.make_async_remote_copy(
            src_ref=src, dst_ref=dst, send_sem=z_send.at[slot], recv_sem=z_recv.at[slot],
            device_id=_at(y, z + dz), device_id_type=MESH,
        )

    def nothing(b, span):
        return jnp.zeros((rows, TB), jnp.float32)

    def into(ref, lo=0):
        def put(b, span, acc):
            ref[b - lo, span] = acc.astype(jnp.bfloat16)

        return put

    def arrive(k):
        if k + 3 < NZ:
            send(k + 3)
        for dy in range(1, NY):
            sends[dy, k].wait_recv()

    hops = []
    arrive(0)
    total(0, 0, half, nothing, into(sp4))
    hops.append(hop(sp4, rp3, 0, 1))
    hops[-1].start()
    total(0, half, half, nothing, into(sm4, half))
    hops.append(hop(sm4, rm3, 1, -1))
    hops[-1].start()
    finish(over_y)
    wz[z] = summed(wy, NY)
    over_z = tell(peers_z, [wz.at[z]] * (NZ - 1), wz.at[z], wz_send, wz_recv)

    def tail(ref, lo):
        def arrived(b, span):
            if lo <= b < lo + half:
                return ref[b - lo, span].astype(jnp.float32)
            return nothing(b, span)

        return arrived

    def whole(ref):
        return lambda b, span: ref[b, span].astype(jnp.float32)

    plan = (
        (rp3, sp3, rp2, 1), (rm3, sm3, rm2, -1),
        (rp2, sp2, rp1, 1), (rm2, sm2, rm1, -1),
        (rp1, sp1, rp0, 1), (rm1, sm1, rm0, -1),
    )
    for i, (got, out, there, dz) in enumerate(plan):
        k = i + 1
        if i == 3:
            finish(over_z)
            w_grad[rows_of(f)] = summed(wz, NZ) * W_SCALE
            back = tell(
                peers_f, [w_grad.at[rows_of(f)]] * (NF - 1), w_grad.at[rows_of(f)], wg_send, wg_recv
            )
        arrive(k)
        hops[i].wait_recv()
        if i < 2:
            arrived = tail(got, 0 if dz == 1 else half)
        else:
            arrived = whole(got)
        total(k, 0, BLK, arrived, into(out))
        hops.append(hop(out, there, i + 2, dz))
        hops[-1].start()
    arrive(7)

    hops[6].wait_recv()
    hops[7].wait_recv()

    def last(b, span):
        return (
            local_part[b, span]
            + rp0[b, span].astype(jnp.float32)
            + rm0[b, span].astype(jnp.float32)
        )

    def put_last(b, span, acc):
        h_sum[b, span] = acc

    total(7, 0, BLK, last, put_last)
    finish(back)
    stores = [pltpu.make_async_copy(w_grad, w_grad_h, out_sem.at[BLK])]
    stores[0].start()
    for b in range(BLK):
        h_grad[b] = h_sum[b].T.astype(jnp.bfloat16)
        stores.append(pltpu.make_async_copy(h_grad.at[b], h_grad_h.at[b], out_sem.at[b]))
        stores[-1].start()
    for copy in stores:
        copy.wait()
    for copy in hops:
        copy.wait_send()
    for copy in sends.values():
        copy.wait_send()


def scatter(contrib, local_part, w_local, need, peer_need):
    hbm = pl.BlockSpec(memory_space=pl.ANY)
    bf = jnp.bfloat16
    blocks = [BLK // 2] * 2 + [BLK] * 6 + [BLK // 2] * 2 + [BLK] * 6
    return pl.pallas_call(
        scatter_kernel,
        out_shape=(
            jax.ShapeDtypeStruct((BLK, TB, TB), bf),
            jax.ShapeDtypeStruct((TB, TB), jnp.float32),
        ),
        in_specs=[hbm] * 5,
        out_specs=(hbm, hbm),
        scratch_shapes=[
            VMEM((BLK, TB, TB), jnp.float32),
            VMEM((TB, TB), jnp.float32),
            SMEM((1, SLOT, NY * NZ), jnp.int32),
            SMEM((NY - 1, 1, SLOT, NY * NZ), jnp.int32),
            VMEM((BLK, TB, TB), bf),
            VMEM((TB, TB), jnp.float32),
            VMEM((NY - 1, NZ, SLOT, TB, TB), bf),
            VMEM((NZ * SLOT, TB, TB), bf),
        ]
        + [VMEM((n, TB, TB), bf) for n in blocks]
        + [VMEM((BLK, TB, TB), jnp.float32)]
        + [VMEM((n, TB // NF, TB), jnp.float32) for n in (NF, NY, NZ)]
        + [DMA, DMA((NY - 1, NZ)), DMA((NY - 1, NZ)), DMA((8,)), DMA((8,))]
        + [DMA((4,)), DMA((BLK + 1,))]
        + [DMA((n - 1,)) for n in (NF, NF, NY, NY, NZ, NZ, NF, NF)],
        compiler_params=pltpu.CompilerParams(
            collective_id=1, has_side_effects=True, vmem_limit_bytes=60 * 2**20
        ),
    )(contrib, local_part, w_local, need, peer_need)


def body(node_feats, cached_feats, tile_values, tile_row, tile_col, tile_count, need_blocks, weights, grad_out):
    node = node_feats.reshape(BLK, TB, TB)
    cached = cached_feats.reshape(SRC - BLK, TB, TB)
    need = jnp.swapaxes(need_blocks, 1, 2)
    gathered, peer_need = gather(node, cached, need)
    output, contrib, local_part, w_local = layer(
        tile_row, tile_col, tile_count, tile_values, node, cached, gathered, weights,
        grad_out.reshape(BLK, TB, TB),
    )
    h_grad, w_grad = scatter(contrib, local_part, w_local, need, peer_need)
    return output.reshape(BLK * TB, TB), h_grad.reshape(BLK * TB, TB), w_grad


def solution(mesh):
    rows = P(("dom", "feat"), None)
    cubes = P(("dom", "feat"), None, None)
    in_specs = (rows, rows, cubes, rows, rows, P(("dom", "feat")), cubes, P(), rows)
    out_specs = (rows, rows, P())
    return jax.shard_map(body, mesh=mesh, in_specs=in_specs, out_specs=out_specs, check_vma=False)
```

```python
import functools
import math

import jax
import jax.numpy as jnp
from jax import lax
from jax.experimental import pallas as pl
from jax.experimental.pallas import tpu as pltpu
from jax.sharding import PartitionSpec as P

MESH = pl.DeviceIdType.MESH
VMEM = pltpu.VMEM
SMEM = pltpu.SMEM
DMA = pltpu.SemaphoreType.DMA
NY = 4
NZ = 8
TB = 128
SRC = 12
BLK = 8
SLOT = 2
NSLOT = NY * NZ * SLOT
NF = 8
PIECE = TB // NF
W_SCALE = 1.0 / math.sqrt(BLK * TB * NY * NZ * NF)
GROUP = 32
CAST = 8


def _place():
    me = lax.axis_index("dom")
    return me // NZ, lax.rem(me, NZ)


def _at(y, z):
    return {"dom": lax.rem(y + NY, NY) * NZ + lax.rem(z + NZ, NZ)}


def _barrier(loads, peers):
    sem = pltpu.get_barrier_semaphore()
    for peer in peers:
        pl.semaphore_signal(sem, inc=1, device_id=peer, device_id_type=MESH)
    for copy in loads:
        copy.start()
    pl.semaphore_wait(sem, len(peers))


NEAR = (0, -1, 1, -2, 2)
FAR = tuple((2, dy) for dy in (0, 1)) + tuple((-2, dy) for dy in (2, 3))
FAR += tuple((dz, dy) for dy in range(NY) for dz in (1, -1))


def gather_kernel(
    node, cached, need, gathered, peer_need,
    own, need_s, zp0, zm0, zp1, zm1, stage, far_stage, pn_v, pn_s, fn_v, fn_s,
    in_sem, need_send, need_recv, far_send, far_recv, pn_sem, fn_sem, out_sem,
    z_send, z_recv, y_send, y_recv, keep_sem, f_send, f_recv,
):
    y, z = _place()
    loads = [
        pltpu.make_async_copy(node, own.at[pl.ds(0, BLK)], in_sem.at[0]),
        pltpu.make_async_copy(cached, own.at[pl.ds(BLK, SRC - BLK)], in_sem.at[1]),
        pltpu.make_async_copy(need, need_s, in_sem.at[2]),
    ]
    offsets = [(dy, 0) for dy in range(1, NY)]
    offsets += [(dy, dz) for dz in (1, -1) for dy in range(NY)]
    offsets += [(dy, 2) for dy in (0, 1, 2)] + [(dy, -2) for dy in (0, 2, 3)]
    _barrier(loads, [_at(y + dy, z + dz) for dy, dz in offsets])
    for copy in loads[:2]:
        copy.wait()
    half = SRC // 2
    parts = pl.ds(0, half), pl.ds(half, half)

    def chain(stops, slot, dz):
        return [
            [
                pltpu.make_async_remote_copy(
                    src_ref=stops[i].at[part], dst_ref=stops[i + 1].at[part],
                    send_sem=z_send.at[slot + 2 * i + n], recv_sem=z_recv.at[slot + 2 * i + n],
                    device_id=_at(y, z + dz), device_id_type=MESH,
                )
                for n, part in enumerate(parts)
            ]
            for i in range(2)
        ]

    up = chain((own, zp0, zp1), 0, 1)
    down = chain((own, zm0, zm1), 4, -1)
    for n in range(2):
        up[0][n].start()
        down[0][n].start()
    asks = [
        pltpu.make_async_remote_copy(
            src_ref=need, dst_ref=pn_v.at[dy - 1],
            send_sem=need_send.at[dy - 1], recv_sem=need_recv.at[dy - 1],
            device_id=_at(y + dy, z), device_id_type=MESH,
        )
        for dy in range(1, NY)
    ]
    far_asks = [
        pltpu.make_async_remote_copy(
            src_ref=need, dst_ref=fn_v.at[i], send_sem=far_send.at[i], recv_sem=far_recv.at[i],
            device_id=_at(y - dy, z - dz), device_id_type=MESH,
        )
        for i, (dz, dy) in enumerate(FAR)
    ]
    for copy in asks + far_asks:
        copy.start()
    loads[2].wait()
    for copy in asks:
        copy.wait()
    to_scalar = pltpu.make_async_copy(pn_v, pn_s, pn_sem)
    to_scalar.start()
    to_output = pltpu.make_async_copy(pn_v, peer_need, out_sem)
    to_output.start()
    to_scalar.wait()

    def slots(y0, z0):
        return pl.ds((lax.rem(y0 + NY, NY) * NZ + lax.rem(z0 + NZ, NZ)) * SLOT, SLOT)

    sends = []
    keeps = []

    def serve(buf, k):
        z0 = lax.rem(z + NEAR[k] + NZ, NZ)
        for dy in range(1, NY):
            for s in range(SLOT):
                stage[dy, k, s] = buf[pn_s[NY - 1 - dy, 0, s, y * NZ + z0]]
            copy = pltpu.make_async_remote_copy(
                src_ref=stage.at[dy, k], dst_ref=gathered.at[slots(y, z0)],
                send_sem=y_send.at[dy - 1, k], recv_sem=y_recv.at[dy - 1, k],
                device_id=_at(y + dy, z), device_id_type=MESH,
            )
            copy.start()
            sends.append((dy, k, copy))
        for s in range(SLOT):
            stage[0, k, s] = buf[need_s[0, s, y * NZ + z0]]
        copy = pltpu.make_async_copy(stage.at[0, k], gathered.at[slots(y, z0)], keep_sem.at[k])
        copy.start()
        keeps.append(copy)

    serve(own, 0)
    for n in range(2):
        up[0][n].wait_recv()
        up[1][n].start()
        down[0][n].wait_recv()
        down[1][n].start()
    serve(zp0, 1)
    serve(zm0, 2)
    for copy in far_asks:
        copy.wait()
    to_scalar = pltpu.make_async_copy(fn_v, fn_s, fn_sem)
    to_scalar.start()
    to_scalar.wait()
    for n in range(2):
        up[1][n].wait_recv()
        down[1][n].wait_recv()
    far_sends = []
    for i, (dz, dy) in enumerate(FAR):
        buf, back = (zp1, -2) if dz > 0 else (zm1, 2)
        z0 = lax.rem(z + back + NZ, NZ)
        for s in range(SLOT):
            far_stage[i, s] = buf[fn_s[i, 0, s, y * NZ + z0]]
        copy = pltpu.make_async_remote_copy(
            src_ref=far_stage.at[i], dst_ref=gathered.at[slots(y, z0)],
            send_sem=f_send.at[i], recv_sem=f_recv.at[i],
            device_id=_at(y + dy, z + dz), device_id_type=MESH,
        )
        copy.start()
        far_sends.append(copy)
    serve(zp1, 3)
    serve(zm1, 4)
    for pairs in up + down:
        for copy in pairs:
            copy.wait_send()
    to_output.wait()
    for copy in keeps:
        copy.wait()
    for dy, k, copy in sends:
        copy.wait_send()
        pltpu.make_async_remote_copy(
            src_ref=stage.at[dy, k], dst_ref=gathered.at[slots(y - dy, z + NEAR[k])],
            send_sem=y_send.at[dy - 1, k], recv_sem=y_recv.at[dy - 1, k],
            device_id=_at(y - dy, z), device_id_type=MESH,
        ).wait_recv()
    for i, (dz, dy) in enumerate(FAR):
        far_sends[i].wait_send()
        back = -2 if dz > 0 else 2
        pltpu.make_async_remote_copy(
            src_ref=far_stage.at[i], dst_ref=gathered.at[slots(y - dy, z - dz + back)],
            send_sem=f_send.at[i], recv_sem=f_recv.at[i],
            device_id=_at(y - dy, z - dz), device_id_type=MESH,
        ).wait_recv()


def gather(node, cached, need):
    block = (SRC, TB, TB)
    return pl.pallas_call(
        gather_kernel,
        out_shape=(
            jax.ShapeDtypeStruct((NSLOT, TB, TB), jnp.bfloat16),
            jax.ShapeDtypeStruct((NY - 1, 1, SLOT, NY * NZ), jnp.int32),
        ),
        in_specs=[pl.BlockSpec(memory_space=pl.ANY)] * 3,
        out_specs=(pl.BlockSpec(memory_space=pl.ANY),) * 2,
        scratch_shapes=[
            VMEM(block, jnp.bfloat16),
            SMEM((1, SLOT, NY * NZ), jnp.int32),
            VMEM(block, jnp.bfloat16),
            VMEM(block, jnp.bfloat16),
            VMEM(block, jnp.bfloat16),
            VMEM(block, jnp.bfloat16),
            VMEM((NY, len(NEAR), SLOT, TB, TB), jnp.bfloat16),
            VMEM((len(FAR), SLOT, TB, TB), jnp.bfloat16),
            VMEM((NY - 1, 1, SLOT, NY * NZ), jnp.int32),
            SMEM((NY - 1, 1, SLOT, NY * NZ), jnp.int32),
            VMEM((len(FAR), 1, SLOT, NY * NZ), jnp.int32),
            SMEM((len(FAR), 1, SLOT, NY * NZ), jnp.int32),
            DMA((3,)),
            DMA((NY - 1,)),
            DMA((NY - 1,)),
            DMA((len(FAR),)),
            DMA((len(FAR),)),
            DMA,
            DMA,
            DMA,
            DMA((8,)),
            DMA((8,)),
            DMA((NY - 1, len(NEAR))),
            DMA((NY - 1, len(NEAR))),
            DMA((len(NEAR),)),
            DMA((len(FAR),)),
            DMA((len(FAR),)),
        ],
        compiler_params=pltpu.CompilerParams(
            collective_id=0, has_side_effects=True, vmem_limit_bytes=60 * 2**20
        ),
    )(node, cached, need)


def layer_kernel(
    row_h, col_h, count_h, tiles_h, node, cached, gathered, weights_h, grad_out_h,
    output_h, contrib_h, local_h, w_local_h,
    row, col, count, weights, grad_out, output, contrib, w_local,
    tiles, table, mixed_acc, grads_t, spread, tile_sem, in_sem, out_sem, spread_sem,
):
    index_loads = [
        pltpu.make_async_copy(src, dst, in_sem.at[i])
        for i, (src, dst) in enumerate(((count_h, count), (row_h, row), (col_h, col)))
    ]
    table_loads = [
        pltpu.make_async_copy(gathered, table.at[pl.ds(SRC, NSLOT)], in_sem.at[3]),
        pltpu.make_async_copy(node, table.at[pl.ds(0, BLK)], in_sem.at[4]),
        pltpu.make_async_copy(cached, table.at[pl.ds(BLK, SRC - BLK)], in_sem.at[5]),
    ]
    dense_loads = [
        pltpu.make_async_copy(weights_h, weights, in_sem.at[6]),
        pltpu.make_async_copy(grad_out_h, grad_out, in_sem.at[7]),
    ]
    for copy in index_loads + table_loads:
        copy.start()

    def tile_load(i):
        span = pl.ds(i * GROUP, GROUP)
        return pltpu.make_async_copy(tiles_h.at[span], tiles.at[span], tile_sem.at[i])

    index_loads[0].wait()
    used = count[0]
    groups = (used + GROUP - 1) // GROUP

    def start_tiles(i, _):
        tile_load(i).start()
        return 0

    lax.fori_loop(0, groups, start_tiles, 0)
    for copy in dense_loads:
        copy.start()
    zero_src = SRC + NSLOT
    table[zero_src] = jnp.zeros((TB, TB), jnp.bfloat16)
    grads_t[BLK] = jnp.zeros((TB, TB), jnp.bfloat16)
    mixed_acc[...] = jnp.zeros_like(mixed_acc)

    def clear(c, _):
        spread[c] = jnp.zeros((TB, TB), jnp.float32)
        return 0

    lax.fori_loop(0, SRC + NSLOT, clear, 0)
    for copy in index_loads[1:] + table_loads:
        copy.wait()

    def forward_step(i, _):
        tile_load(i).wait()
        products = []
        for u in range(GROUP):
            t = i * GROUP + u
            c = jnp.where(t < used, col[0, t], zero_src)
            products.append(jnp.dot(tiles[t], table[c], preferred_element_type=jnp.float32))
        for u in range(GROUP):
            r = row[0, i * GROUP + u]
            mixed_acc[r] += products[u]
        return 0

    lax.fori_loop(0, groups, forward_step, 0)
    for copy in dense_loads:
        copy.wait()

    w = weights[...]
    w_sum = jnp.zeros((TB, TB), jnp.float32)
    for r in range(BLK):
        mixed = mixed_acc[r].astype(jnp.bfloat16)
        pre = jnp.dot(mixed, w, preferred_element_type=jnp.float32)
        sig = jax.nn.sigmoid(pre)
        output[r] = (pre * sig).astype(jnp.bfloat16)
        act = (grad_out[r].astype(jnp.float32) * sig * (1.0 + pre * (1.0 - sig))).astype(jnp.bfloat16)
        grads_t[r] = lax.dot_general(
            w, act, (((1,), (1,)), ((), ())), preferred_element_type=jnp.float32
        ).astype(jnp.bfloat16)
        w_sum += lax.dot_general(
            mixed, act, (((0,), (0,)), ((), ())), preferred_element_type=jnp.float32
        )
    w_local[...] = w_sum
    stores = [
        pltpu.make_async_copy(output, output_h, out_sem.at[0]),
        pltpu.make_async_copy(w_local, w_local_h, out_sem.at[1]),
    ]
    for copy in stores:
        copy.start()

    def backward_step(i, _):
        products = []
        for u in range(GROUP):
            t = i * GROUP + u
            r = jnp.where(t < used, row[0, t], BLK)
            products.append(jnp.dot(grads_t[r], tiles[t], preferred_element_type=jnp.float32))
        for u in range(GROUP):
            c = col[0, i * GROUP + u]
            spread[c] += products[u]
        return 0

    lax.fori_loop(0, groups, backward_step, 0)
    stores.append(pltpu.make_async_copy(spread.at[pl.ds(0, BLK)], local_h, out_sem.at[2]))
    stores[-1].start()

    def store_part(i):
        span = pl.ds(i * CAST, CAST)
        return pltpu.make_async_copy(contrib.at[span], contrib_h.at[span], spread_sem.at[i])

    def cast(i, _):
        for u in range(CAST):
            s = i * CAST + u
            contrib[s] = spread[SRC + s].astype(jnp.bfloat16)
        store_part(i).start()
        return 0

    lax.fori_loop(0, NSLOT // CAST, cast, 0)
    for i in range(NSLOT // CAST):
        store_part(i).wait()
    for copy in stores:
        copy.wait()


def layer(row, col, count, tiles, node, cached, gathered, weights, grad_out):
    cap = tiles.shape[0]
    flops = 4 * cap * TB**3
    hbm = pl.BlockSpec(memory_space=pl.ANY)
    bf, f32 = jnp.bfloat16, jnp.float32
    return pl.pallas_call(
        layer_kernel,
        out_shape=(
            jax.ShapeDtypeStruct((BLK, TB, TB), bf),
            jax.ShapeDtypeStruct((NSLOT, TB, TB), bf),
            jax.ShapeDtypeStruct((BLK, TB, TB), f32),
            jax.ShapeDtypeStruct((TB, TB), f32),
        ),
        in_specs=[hbm] * 9,
        out_specs=(hbm,) * 4,
        scratch_shapes=[
            SMEM((1, cap), jnp.int32),
            SMEM((1, cap), jnp.int32),
            SMEM((1,), jnp.int32),
            VMEM((TB, TB), bf),
            VMEM((BLK, TB, TB), bf),
            VMEM((BLK, TB, TB), bf),
            VMEM((NSLOT, TB, TB), bf),
            VMEM((TB, TB), f32),
            VMEM((cap, TB, TB), bf),
            VMEM((SRC + NSLOT + 1, TB, TB), bf),
            VMEM((BLK, TB, TB), f32),
            VMEM((BLK + 1, TB, TB), bf),
            VMEM((SRC + NSLOT, TB, TB), f32),
            DMA((cap // GROUP,)),
            DMA((8,)),
            DMA((3,)),
            DMA((NSLOT // CAST,)),
        ],
        compiler_params=pltpu.CompilerParams(vmem_limit_bytes=60 * 2**20),
        cost_estimate=pl.CostEstimate(
            flops=flops, bytes_accessed=16 * 2**20, transcendentals=BLK * TB * TB
        ),
    )(row, col, count, tiles, node, cached, gathered, weights, grad_out)


SCATTER_ORDER = (4, 3, -3, 2, -2, 1, -1, 0)


def scatter_kernel(
    contrib, local_h, w_local_h, need_h, peer_need_h, h_grad_h, w_grad_h,
    local_part, w_local, need_s, peer_need, h_grad, w_grad, ybuf, ownc, sp4, sm4, sp3, sm3, sp2, sm2, sp1, sm1,
    rp3, rm3, rp2, rm2, rp1, rm1, rp0, rm0, h_sum,
    wf, wy, wz, own_sem, y_send, y_recv, z_send, z_recv,
    load_sem, out_sem, wf_send, wf_recv, wy_send, wy_recv, wz_send, wz_recv, wg_send, wg_recv,
):
    y, z = _place()
    f = lax.axis_index("feat")
    mine = pltpu.make_async_copy(contrib.at[pl.ds(y * NZ * SLOT, NZ * SLOT)], ownc, own_sem)
    loads = [
        pltpu.make_async_copy(src, dst, load_sem.at[i])
        for i, (src, dst) in enumerate(
            (
                (w_local_h, w_local), (local_h, local_part),
                (need_h, need_s), (peer_need_h, peer_need),
            )
        )
    ]
    peers_f = [{"feat": lax.rem(f + df, NF)} for df in range(1, NF)]
    peers_y = [_at(y + dy, z) for dy in range(1, NY)]
    peers_z = [_at(y, z + dz) for dz in range(1, NZ)]
    _barrier([mine] + loads, peers_f + peers_y + peers_z)
    piece = PIECE

    def rows_of(i):
        return pl.ds(pl.multiple_of(i * piece, piece), piece)

    def tell(peers, srcs, dst, send_sem, recv_sem):
        copies = [
            pltpu.make_async_remote_copy(
                src_ref=src, dst_ref=dst, send_sem=send_sem.at[i], recv_sem=recv_sem.at[i],
                device_id=peer, device_id_type=MESH,
            )
            for i, (peer, src) in enumerate(zip(peers, srcs))
        ]
        for copy in copies:
            copy.start()
        return copies

    def finish(copies):
        for copy in copies:
            copy.wait()

    def summed(ref, n):
        acc = ref[0]
        for i in range(1, n):
            acc = acc + ref[i]
        return acc

    loads[0].wait()
    wf[f] = w_local[rows_of(f)]
    over_f = tell(
        peers_f, [w_local.at[rows_of(p["feat"])] for p in peers_f], wf.at[f], wf_send, wf_recv
    )
    sends = {}

    def send(k):
        z0 = lax.rem(z + SCATTER_ORDER[k] + NZ, NZ)
        for dy in range(1, NY):
            theirs = (lax.rem(y + dy, NY) * NZ + z0) * SLOT
            copy = pltpu.make_async_remote_copy(
                src_ref=contrib.at[pl.ds(theirs, SLOT)], dst_ref=ybuf.at[dy - 1, k],
                send_sem=y_send.at[dy - 1, k], recv_sem=y_recv.at[dy - 1, k],
                device_id=_at(y + dy, z), device_id_type=MESH,
            )
            copy.start()
            sends[dy, k] = copy

    for k in range(NZ):
        send(k)
    for copy in [mine] + loads[1:]:
        copy.wait()
    half = BLK // 2
    rows = 32

    def total(k, lo, n, arrived, put):
        z0 = lax.rem(z + SCATTER_ORDER[k] + NZ, NZ)
        ids = [need_s[0, s, y * NZ + z0] for s in range(SLOT)]
        for dy in range(1, NY):
            ids += [peer_need[dy - 1, 0, s, y * NZ + z0] for s in range(SLOT)]

        def part(i, _):
            span = pl.ds(pl.multiple_of(i * rows, rows), rows)
            parts = [ownc[z0 * SLOT + s, span] for s in range(SLOT)]
            for dy in range(1, NY):
                parts += [ybuf[dy - 1, k, s, span] for s in range(SLOT)]
            parts = [p.astype(jnp.float32) for p in parts]
            for b in range(lo, lo + n):
                acc = arrived(b, span)
                for p, which in zip(parts, ids):
                    acc = acc + jnp.where(which == b, p, 0.0)
                put(b, span, acc)
            return 0

        lax.fori_loop(0, TB // rows, part, 0)

    def hop(src, dst, slot, dz):
        return pltpu.make_async_remote_copy(
            src_ref=src, dst_ref=dst, send_sem=z_send.at[slot], recv_sem=z_recv.at[slot],
            device_id=_at(y, z + dz), device_id_type=MESH,
        )

    def nothing(b, span):
        return jnp.zeros((rows, TB), jnp.float32)

    def into(ref, lo=0):
        def put(b, span, acc):
            ref[b - lo, span] = acc.astype(jnp.bfloat16)

        return put

    def arrive(k):
        for dy in range(1, NY):
            sends[dy, k].wait_recv()

    def half_of(ref, n):
        return ref.at[pl.ds(n * half, half)]

    hops = []

    def forward(src, dst, dz):
        hops.append(hop(src, dst, len(hops), dz))
        hops[-1].start()
        return hops[-1]

    finish(over_f)
    wz[z] = summed(wf, NF)
    over_z = tell(peers_z, [wz.at[z]] * (NZ - 1), wz.at[z], wz_send, wz_recv)
    arrive(0)
    total(0, 0, half, nothing, into(sp4))
    coming_up = [forward(sp4, rp3, 1), None]
    total(0, half, half, nothing, into(sm4, half))
    coming_down = [None, forward(sm4, rm3, -1)]

    def whole(ref):
        return lambda b, span: ref[b, span].astype(jnp.float32)

    def far(ref, lo):
        return lambda b, span: ref[b - lo, span].astype(jnp.float32)

    def step(k, coming, got, out, there, dz):
        arrive(k)
        leaving = [None, None]
        for n in (1, 0) if dz == 1 else (0, 1):
            arrived = nothing
            if coming[n] is not None:
                coming[n].wait_recv()
                arrived = whole(got) if k > 2 else far(got, n * half)
            total(k, n * half, half, arrived, into(out))
            leaving[n] = forward(half_of(out, n), half_of(there, n), dz)
        return leaving

    coming_up = step(1, coming_up, rp3, sp3, rp2, 1)
    coming_down = step(2, coming_down, rm3, sm3, rm2, -1)
    finish(over_z)
    wy[y] = summed(wz, NZ)
    over_y = tell(peers_y, [wy.at[y]] * (NY - 1), wy.at[y], wy_send, wy_recv)
    coming_up = step(3, coming_up, rp2, sp2, rp1, 1)
    coming_down = step(4, coming_down, rm2, sm2, rm1, -1)
    coming_up = step(5, coming_up, rp1, sp1, rp0, 1)
    finish(over_y)
    w_grad[rows_of(f)] = summed(wy, NY) * W_SCALE
    back = tell(
        peers_f, [w_grad.at[rows_of(f)]] * (NF - 1), w_grad.at[rows_of(f)], wg_send, wg_recv
    )
    coming_down = step(6, coming_down, rm1, sm1, rm0, -1)
    arrive(7)

    def last(b, span):
        return (
            local_part[b, span]
            + rp0[b, span].astype(jnp.float32)
            + rm0[b, span].astype(jnp.float32)
        )

    def put_last(b, span, acc):
        h_sum[b, span] = acc

    stores = []
    for copy in coming_up + coming_down:
        copy.wait_recv()
    for n in range(2):
        total(7, n * half, half, last, put_last)
        for b in range(n * half, n * half + half):
            h_grad[b] = h_sum[b].T.astype(jnp.bfloat16)
        stores.append(
            pltpu.make_async_copy(half_of(h_grad, n), half_of(h_grad_h, n), out_sem.at[n])
        )
        stores[-1].start()
    for copy in hops:
        copy.wait_send()
    for copy in sends.values():
        copy.wait_send()
    finish(back)
    stores.append(pltpu.make_async_copy(w_grad, w_grad_h, out_sem.at[2]))
    stores[-1].start()
    for copy in stores:
        copy.wait()


def scatter(contrib, local_part, w_local, need, peer_need):
    hbm = pl.BlockSpec(memory_space=pl.ANY)
    bf = jnp.bfloat16
    blocks = [BLK // 2] * 2 + [BLK] * 6 + [BLK // 2] * 2 + [BLK] * 6
    return pl.pallas_call(
        scatter_kernel,
        out_shape=(
            jax.ShapeDtypeStruct((BLK, TB, TB), bf),
            jax.ShapeDtypeStruct((TB, TB), jnp.float32),
        ),
        in_specs=[hbm] * 5,
        out_specs=(hbm, hbm),
        scratch_shapes=[
            VMEM((BLK, TB, TB), jnp.float32),
            VMEM((TB, TB), jnp.float32),
            SMEM((1, SLOT, NY * NZ), jnp.int32),
            SMEM((NY - 1, 1, SLOT, NY * NZ), jnp.int32),
            VMEM((BLK, TB, TB), bf),
            VMEM((TB, TB), jnp.float32),
            VMEM((NY - 1, NZ, SLOT, TB, TB), bf),
            VMEM((NZ * SLOT, TB, TB), bf),
        ]
        + [VMEM((n, TB, TB), bf) for n in blocks]
        + [VMEM((BLK, TB, TB), jnp.float32)]
        + [VMEM((n, PIECE, TB), jnp.float32) for n in (NF, NY, NZ)]
        + [DMA, DMA((NY - 1, NZ)), DMA((NY - 1, NZ)), DMA((14,)), DMA((14,))]
        + [DMA((4,)), DMA((3,))]
        + [DMA((n - 1,)) for n in (NF, NF, NY, NY, NZ, NZ, NF, NF)],
        compiler_params=pltpu.CompilerParams(
            collective_id=1, has_side_effects=True, vmem_limit_bytes=60 * 2**20
        ),
    )(contrib, local_part, w_local, need, peer_need)


def body(node_feats, cached_feats, tile_values, tile_row, tile_col, tile_count, need_blocks, weights, grad_out):
    node = node_feats.reshape(BLK, TB, TB)
    cached = cached_feats.reshape(SRC - BLK, TB, TB)
    need = jnp.swapaxes(need_blocks, 1, 2)
    gathered, peer_need = gather(node, cached, need)
    output, contrib, local_part, w_local = layer(
        tile_row, tile_col, tile_count, tile_values, node, cached, gathered, weights,
        grad_out.reshape(BLK, TB, TB),
    )
    h_grad, w_grad = scatter(contrib, local_part, w_local, need, peer_need)
    return output.reshape(BLK * TB, TB), h_grad.reshape(BLK * TB, TB), w_grad


def solution(mesh):
    rows = P(("dom", "feat"), None)
    cubes = P(("dom", "feat"), None, None)
    in_specs = (rows, rows, cubes, rows, rows, P(("dom", "feat")), cubes, P(), rows)
    out_specs = (rows, rows, P())
    return jax.shard_map(body, mesh=mesh, in_specs=in_specs, out_specs=out_specs, check_vma=False)
```

```python
import functools
import math

import jax
import jax.numpy as jnp
from jax import lax
from jax.experimental import pallas as pl
from jax.experimental.pallas import tpu as pltpu
from jax.sharding import PartitionSpec as P

MESH = pl.DeviceIdType.MESH
VMEM = pltpu.VMEM
SMEM = pltpu.SMEM
DMA = pltpu.SemaphoreType.DMA
NY = 4
NZ = 8
TB = 128
SRC = 12
BLK = 8
SLOT = 2
NSLOT = NY * NZ * SLOT
NF = 8
PIECE = TB // NF
W_SCALE = 1.0 / math.sqrt(BLK * TB * NY * NZ * NF)
GROUP = 32
CAST = 8


def _place():
    me = lax.axis_index("dom")
    return me // NZ, lax.rem(me, NZ)


def _at(y, z):
    return {"dom": lax.rem(y + NY, NY) * NZ + lax.rem(z + NZ, NZ)}


def _barrier(loads, peers):
    sem = pltpu.get_barrier_semaphore()
    for peer in peers:
        pl.semaphore_signal(sem, inc=1, device_id=peer, device_id_type=MESH)
    for copy in loads:
        copy.start()
    pl.semaphore_wait(sem, len(peers))


NEAR = (0, -1, 1, -2, 2)
FAR = tuple((2, dy) for dy in (0, 1)) + tuple((-2, dy) for dy in (2, 3))
FAR += tuple((dz, dy) for dy in range(NY) for dz in (1, -1))


def gather_kernel(
    node, cached, need, gathered, peer_need,
    own, need_s, zp0, zm0, zp1, zm1, stage, far_stage, pn_v, pn_s, fn_v, fn_s,
    in_sem, need_send, need_recv, far_send, far_recv, pn_sem, fn_sem, out_sem,
    z_send, z_recv, y_send, y_recv, keep_sem, f_send, f_recv,
):
    y, z = _place()
    loads = [
        pltpu.make_async_copy(node, own.at[pl.ds(0, BLK)], in_sem.at[0]),
        pltpu.make_async_copy(cached, own.at[pl.ds(BLK, SRC - BLK)], in_sem.at[1]),
        pltpu.make_async_copy(need, need_s, in_sem.at[2]),
    ]
    offsets = [(dy, 0) for dy in range(1, NY)]
    offsets += [(dy, dz) for dz in (1, -1) for dy in range(NY)]
    offsets += [(dy, 2) for dy in (0, 1, 2)] + [(dy, -2) for dy in (0, 2, 3)]
    _barrier(loads, [_at(y + dy, z + dz) for dy, dz in offsets])
    for copy in loads[:2]:
        copy.wait()
    half = SRC // 2
    parts = pl.ds(0, half), pl.ds(half, half)

    def chain(stops, slot, dz):
        return [
            [
                pltpu.make_async_remote_copy(
                    src_ref=stops[i].at[part], dst_ref=stops[i + 1].at[part],
                    send_sem=z_send.at[slot + 2 * i + n], recv_sem=z_recv.at[slot + 2 * i + n],
                    device_id=_at(y, z + dz), device_id_type=MESH,
                )
                for n, part in enumerate(parts)
            ]
            for i in range(2)
        ]

    up = chain((own, zp0, zp1), 0, 1)
    down = chain((own, zm0, zm1), 4, -1)
    for n in range(2):
        up[0][n].start()
        down[0][n].start()
    asks = [
        pltpu.make_async_remote_copy(
            src_ref=need, dst_ref=pn_v.at[dy - 1],
            send_sem=need_send.at[dy - 1], recv_sem=need_recv.at[dy - 1],
            device_id=_at(y + dy, z), device_id_type=MESH,
        )
        for dy in range(1, NY)
    ]
    far_asks = [
        pltpu.make_async_remote_copy(
            src_ref=need, dst_ref=fn_v.at[i], send_sem=far_send.at[i], recv_sem=far_recv.at[i],
            device_id=_at(y - dy, z - dz), device_id_type=MESH,
        )
        for i, (dz, dy) in enumerate(FAR)
    ]
    for copy in asks + far_asks:
        copy.start()
    loads[2].wait()
    for copy in asks:
        copy.wait()
    to_scalar = pltpu.make_async_copy(pn_v, pn_s, pn_sem)
    to_scalar.start()
    to_output = pltpu.make_async_copy(pn_v, peer_need, out_sem)
    to_output.start()
    to_scalar.wait()

    def slots(y0, z0):
        return pl.ds((lax.rem(y0 + NY, NY) * NZ + lax.rem(z0 + NZ, NZ)) * SLOT, SLOT)

    sends = []
    keeps = []

    def serve(buf, k):
        z0 = lax.rem(z + NEAR[k] + NZ, NZ)
        for dy in range(1, NY):
            for s in range(SLOT):
                stage[dy, k, s] = buf[pn_s[NY - 1 - dy, 0, s, y * NZ + z0]]
            copy = pltpu.make_async_remote_copy(
                src_ref=stage.at[dy, k], dst_ref=gathered.at[slots(y, z0)],
                send_sem=y_send.at[dy - 1, k], recv_sem=y_recv.at[dy - 1, k],
                device_id=_at(y + dy, z), device_id_type=MESH,
            )
            copy.start()
            sends.append((dy, k, copy))
        for s in range(SLOT):
            stage[0, k, s] = buf[need_s[0, s, y * NZ + z0]]
        copy = pltpu.make_async_copy(stage.at[0, k], gathered.at[slots(y, z0)], keep_sem.at[k])
        copy.start()
        keeps.append(copy)

    serve(own, 0)
    for n in range(2):
        up[0][n].wait_recv()
        up[1][n].start()
        down[0][n].wait_recv()
        down[1][n].start()
    serve(zp0, 1)
    serve(zm0, 2)
    for copy in far_asks:
        copy.wait()
    to_scalar = pltpu.make_async_copy(fn_v, fn_s, fn_sem)
    to_scalar.start()
    to_scalar.wait()
    for n in range(2):
        up[1][n].wait_recv()
        down[1][n].wait_recv()
    far_sends = []
    for i, (dz, dy) in enumerate(FAR):
        buf, back = (zp1, -2) if dz > 0 else (zm1, 2)
        z0 = lax.rem(z + back + NZ, NZ)
        for s in range(SLOT):
            far_stage[i, s] = buf[fn_s[i, 0, s, y * NZ + z0]]
        copy = pltpu.make_async_remote_copy(
            src_ref=far_stage.at[i], dst_ref=gathered.at[slots(y, z0)],
            send_sem=f_send.at[i], recv_sem=f_recv.at[i],
            device_id=_at(y + dy, z + dz), device_id_type=MESH,
        )
        copy.start()
        far_sends.append(copy)
    serve(zp1, 3)
    serve(zm1, 4)
    for pairs in up + down:
        for copy in pairs:
            copy.wait_send()
    to_output.wait()
    for copy in keeps:
        copy.wait()
    for dy, k, copy in sends:
        copy.wait_send()
        pltpu.make_async_remote_copy(
            src_ref=stage.at[dy, k], dst_ref=gathered.at[slots(y - dy, z + NEAR[k])],
            send_sem=y_send.at[dy - 1, k], recv_sem=y_recv.at[dy - 1, k],
            device_id=_at(y - dy, z), device_id_type=MESH,
        ).wait_recv()
    for i, (dz, dy) in enumerate(FAR):
        far_sends[i].wait_send()
        back = -2 if dz > 0 else 2
        pltpu.make_async_remote_copy(
            src_ref=far_stage.at[i], dst_ref=gathered.at[slots(y - dy, z - dz + back)],
            send_sem=f_send.at[i], recv_sem=f_recv.at[i],
            device_id=_at(y - dy, z - dz), device_id_type=MESH,
        ).wait_recv()


def gather(node, cached, need):
    block = (SRC, TB, TB)
    return pl.pallas_call(
        gather_kernel,
        out_shape=(
            jax.ShapeDtypeStruct((NSLOT, TB, TB), jnp.bfloat16),
            jax.ShapeDtypeStruct((NY - 1, 1, SLOT, NY * NZ), jnp.int32),
        ),
        in_specs=[pl.BlockSpec(memory_space=pl.ANY)] * 3,
        out_specs=(pl.BlockSpec(memory_space=pl.ANY),) * 2,
        scratch_shapes=[
            VMEM(block, jnp.bfloat16),
            SMEM((1, SLOT, NY * NZ), jnp.int32),
            VMEM(block, jnp.bfloat16),
            VMEM(block, jnp.bfloat16),
            VMEM(block, jnp.bfloat16),
            VMEM(block, jnp.bfloat16),
            VMEM((NY, len(NEAR), SLOT, TB, TB), jnp.bfloat16),
            VMEM((len(FAR), SLOT, TB, TB), jnp.bfloat16),
            VMEM((NY - 1, 1, SLOT, NY * NZ), jnp.int32),
            SMEM((NY - 1, 1, SLOT, NY * NZ), jnp.int32),
            VMEM((len(FAR), 1, SLOT, NY * NZ), jnp.int32),
            SMEM((len(FAR), 1, SLOT, NY * NZ), jnp.int32),
            DMA((3,)),
            DMA((NY - 1,)),
            DMA((NY - 1,)),
            DMA((len(FAR),)),
            DMA((len(FAR),)),
            DMA,
            DMA,
            DMA,
            DMA((8,)),
            DMA((8,)),
            DMA((NY - 1, len(NEAR))),
            DMA((NY - 1, len(NEAR))),
            DMA((len(NEAR),)),
            DMA((len(FAR),)),
            DMA((len(FAR),)),
        ],
        compiler_params=pltpu.CompilerParams(
            collective_id=0, has_side_effects=True, vmem_limit_bytes=60 * 2**20
        ),
    )(node, cached, need)


def layer_kernel(
    row_h, col_h, count_h, tiles_h, node, cached, gathered, weights_h, grad_out_h,
    output_h, contrib_h, local_h, w_local_h,
    row, col, count, weights, grad_out, output, contrib, w_local,
    tiles, table, mixed_acc, grads_t, spread, tile_sem, in_sem, out_sem, spread_sem,
):
    index_loads = [
        pltpu.make_async_copy(src, dst, in_sem.at[i])
        for i, (src, dst) in enumerate(((count_h, count), (row_h, row), (col_h, col)))
    ]
    table_loads = [
        pltpu.make_async_copy(gathered, table.at[pl.ds(SRC, NSLOT)], in_sem.at[3]),
        pltpu.make_async_copy(node, table.at[pl.ds(0, BLK)], in_sem.at[4]),
        pltpu.make_async_copy(cached, table.at[pl.ds(BLK, SRC - BLK)], in_sem.at[5]),
    ]
    dense_loads = [
        pltpu.make_async_copy(weights_h, weights, in_sem.at[6]),
        pltpu.make_async_copy(grad_out_h, grad_out, in_sem.at[7]),
    ]
    for copy in index_loads + table_loads:
        copy.start()

    def tile_load(i):
        span = pl.ds(i * GROUP, GROUP)
        return pltpu.make_async_copy(tiles_h.at[span], tiles.at[span], tile_sem.at[i])

    index_loads[0].wait()
    used = count[0]
    groups = (used + GROUP - 1) // GROUP

    def start_tiles(i, _):
        tile_load(i).start()
        return 0

    lax.fori_loop(0, groups, start_tiles, 0)
    for copy in dense_loads:
        copy.start()
    zero_src = SRC + NSLOT
    table[zero_src] = jnp.zeros((TB, TB), jnp.bfloat16)
    grads_t[BLK] = jnp.zeros((TB, TB), jnp.bfloat16)
    mixed_acc[...] = jnp.zeros_like(mixed_acc)

    def clear(c, _):
        spread[c] = jnp.zeros((TB, TB), jnp.float32)
        return 0

    lax.fori_loop(0, SRC + NSLOT, clear, 0)
    for copy in index_loads[1:] + table_loads:
        copy.wait()

    def forward_step(i, _):
        tile_load(i).wait()
        products = []
        for u in range(GROUP):
            t = i * GROUP + u
            c = jnp.where(t < used, col[0, t], zero_src)
            products.append(jnp.dot(tiles[t], table[c], preferred_element_type=jnp.float32))
        for u in range(GROUP):
            r = row[0, i * GROUP + u]
            mixed_acc[r] += products[u]
        return 0

    lax.fori_loop(0, groups, forward_step, 0)
    for copy in dense_loads:
        copy.wait()

    w = weights[...]
    w_sum = jnp.zeros((TB, TB), jnp.float32)
    for r in range(BLK):
        mixed = mixed_acc[r].astype(jnp.bfloat16)
        pre = jnp.dot(mixed, w, preferred_element_type=jnp.float32)
        sig = jax.nn.sigmoid(pre)
        output[r] = (pre * sig).astype(jnp.bfloat16)
        act = (grad_out[r].astype(jnp.float32) * sig * (1.0 + pre * (1.0 - sig))).astype(jnp.bfloat16)
        grads_t[r] = lax.dot_general(
            w, act, (((1,), (1,)), ((), ())), preferred_element_type=jnp.float32
        ).astype(jnp.bfloat16)
        w_sum += lax.dot_general(
            mixed, act, (((0,), (0,)), ((), ())), preferred_element_type=jnp.float32
        )
    w_local[...] = w_sum
    stores = [
        pltpu.make_async_copy(output, output_h, out_sem.at[0]),
        pltpu.make_async_copy(w_local, w_local_h, out_sem.at[1]),
    ]
    for copy in stores:
        copy.start()

    def backward_step(i, _):
        products = []
        for u in range(GROUP):
            t = i * GROUP + u
            r = jnp.where(t < used, row[0, t], BLK)
            products.append(jnp.dot(grads_t[r], tiles[t], preferred_element_type=jnp.float32))
        for u in range(GROUP):
            c = col[0, i * GROUP + u]
            spread[c] += products[u]
        return 0

    lax.fori_loop(0, groups, backward_step, 0)
    stores.append(pltpu.make_async_copy(spread.at[pl.ds(0, BLK)], local_h, out_sem.at[2]))
    stores[-1].start()

    def store_part(i):
        span = pl.ds(i * CAST, CAST)
        return pltpu.make_async_copy(contrib.at[span], contrib_h.at[span], spread_sem.at[i])

    def cast(i, _):
        for u in range(CAST):
            s = i * CAST + u
            contrib[s] = spread[SRC + s].astype(jnp.bfloat16)
        store_part(i).start()
        return 0

    lax.fori_loop(0, NSLOT // CAST, cast, 0)
    for i in range(NSLOT // CAST):
        store_part(i).wait()
    for copy in stores:
        copy.wait()


def layer(row, col, count, tiles, node, cached, gathered, weights, grad_out):
    cap = tiles.shape[0]
    flops = 4 * cap * TB**3
    hbm = pl.BlockSpec(memory_space=pl.ANY)
    bf, f32 = jnp.bfloat16, jnp.float32
    return pl.pallas_call(
        layer_kernel,
        out_shape=(
            jax.ShapeDtypeStruct((BLK, TB, TB), bf),
            jax.ShapeDtypeStruct((NSLOT, TB, TB), bf),
            jax.ShapeDtypeStruct((BLK, TB, TB), f32),
            jax.ShapeDtypeStruct((TB, TB), f32),
        ),
        in_specs=[hbm] * 9,
        out_specs=(hbm,) * 4,
        scratch_shapes=[
            SMEM((1, cap), jnp.int32),
            SMEM((1, cap), jnp.int32),
            SMEM((1,), jnp.int32),
            VMEM((TB, TB), bf),
            VMEM((BLK, TB, TB), bf),
            VMEM((BLK, TB, TB), bf),
            VMEM((NSLOT, TB, TB), bf),
            VMEM((TB, TB), f32),
            VMEM((cap, TB, TB), bf),
            VMEM((SRC + NSLOT + 1, TB, TB), bf),
            VMEM((BLK, TB, TB), f32),
            VMEM((BLK + 1, TB, TB), bf),
            VMEM((SRC + NSLOT, TB, TB), f32),
            DMA((cap // GROUP,)),
            DMA((8,)),
            DMA((3,)),
            DMA((NSLOT // CAST,)),
        ],
        compiler_params=pltpu.CompilerParams(vmem_limit_bytes=60 * 2**20),
        cost_estimate=pl.CostEstimate(
            flops=flops, bytes_accessed=16 * 2**20, transcendentals=BLK * TB * TB
        ),
    )(row, col, count, tiles, node, cached, gathered, weights, grad_out)


SCATTER_ORDER = (4, 3, -3, 2, -2, 1, -1, 0)


def scatter_kernel(
    contrib, local_h, w_local_h, need_h, peer_need_h, h_grad_h, w_grad_h,
    local_part, w_local, need_s, peer_need, h_grad, w_grad, ybuf, ownc, sp4, sm4, sp3, sm3, sp2, sm2, sp1, sm1,
    rp3, rm3, rp2, rm2, rp1, rm1, rp0, rm0, h_sum,
    wf, wy, wz, own_sem, y_send, y_recv, z_send, z_recv,
    load_sem, out_sem, wf_send, wf_recv, wy_send, wy_recv, wz_send, wz_recv, wg_send, wg_recv,
):
    y, z = _place()
    f = lax.axis_index("feat")
    mine = pltpu.make_async_copy(contrib.at[pl.ds(y * NZ * SLOT, NZ * SLOT)], ownc, own_sem)
    loads = [
        pltpu.make_async_copy(src, dst, load_sem.at[i])
        for i, (src, dst) in enumerate(
            (
                (w_local_h, w_local), (local_h, local_part),
                (need_h, need_s), (peer_need_h, peer_need),
            )
        )
    ]
    peers_f = [{"feat": lax.rem(f + df, NF)} for df in range(1, NF)]
    peers_y = [_at(y + dy, z) for dy in range(1, NY)]
    peers_z = [_at(y, z + dz) for dz in range(1, NZ)]
    _barrier([mine] + loads, peers_f + peers_y + peers_z)
    piece = PIECE

    def rows_of(i):
        return pl.ds(pl.multiple_of(i * piece, piece), piece)

    def tell(peers, srcs, dst, send_sem, recv_sem):
        copies = [
            pltpu.make_async_remote_copy(
                src_ref=src, dst_ref=dst, send_sem=send_sem.at[i], recv_sem=recv_sem.at[i],
                device_id=peer, device_id_type=MESH,
            )
            for i, (peer, src) in enumerate(zip(peers, srcs))
        ]
        for copy in copies:
            copy.start()
        return copies

    def finish(copies):
        for copy in copies:
            copy.wait()

    def summed(ref, n):
        acc = ref[0]
        for i in range(1, n):
            acc = acc + ref[i]
        return acc

    loads[0].wait()
    wf[f] = w_local[rows_of(f)]
    over_f = tell(
        peers_f, [w_local.at[rows_of(p["feat"])] for p in peers_f], wf.at[f], wf_send, wf_recv
    )
    sends = {}

    def send(k):
        z0 = lax.rem(z + SCATTER_ORDER[k] + NZ, NZ)
        for dy in range(1, NY):
            theirs = (lax.rem(y + dy, NY) * NZ + z0) * SLOT
            copy = pltpu.make_async_remote_copy(
                src_ref=contrib.at[pl.ds(theirs, SLOT)], dst_ref=ybuf.at[dy - 1, k],
                send_sem=y_send.at[dy - 1, k], recv_sem=y_recv.at[dy - 1, k],
                device_id=_at(y + dy, z), device_id_type=MESH,
            )
            copy.start()
            sends[dy, k] = copy

    for k in range(NZ):
        send(k)
    for copy in [mine] + loads[1:]:
        copy.wait()
    half = BLK // 2
    rows = 32

    def total(k, lo, n, arrived, put):
        z0 = lax.rem(z + SCATTER_ORDER[k] + NZ, NZ)
        ids = [need_s[0, s, y * NZ + z0] for s in range(SLOT)]
        for dy in range(1, NY):
            ids += [peer_need[dy - 1, 0, s, y * NZ + z0] for s in range(SLOT)]

        def part(i, _):
            span = pl.ds(pl.multiple_of(i * rows, rows), rows)
            parts = [ownc[z0 * SLOT + s, span] for s in range(SLOT)]
            for dy in range(1, NY):
                parts += [ybuf[dy - 1, k, s, span] for s in range(SLOT)]
            parts = [p.astype(jnp.float32) for p in parts]
            for b in range(lo, lo + n):
                acc = arrived(b, span)
                for p, which in zip(parts, ids):
                    acc = acc + jnp.where(which == b, p, 0.0)
                put(b, span, acc)
            return 0

        lax.fori_loop(0, TB // rows, part, 0)

    def hop(src, dst, slot, dz):
        return pltpu.make_async_remote_copy(
            src_ref=src, dst_ref=dst, send_sem=z_send.at[slot], recv_sem=z_recv.at[slot],
            device_id=_at(y, z + dz), device_id_type=MESH,
        )

    def nothing(b, span):
        return jnp.zeros((rows, TB), jnp.float32)

    def into(ref, lo=0):
        def put(b, span, acc):
            ref[b - lo, span] = acc.astype(jnp.bfloat16)

        return put

    def arrive(k):
        for dy in range(1, NY):
            sends[dy, k].wait_recv()

    def half_of(ref, n):
        return ref.at[pl.ds(n * half, half)]

    hops = []

    def forward(src, dst, dz):
        hops.append(hop(src, dst, len(hops), dz))
        hops[-1].start()
        return hops[-1]

    finish(over_f)
    wz[z] = summed(wf, NF)
    over_z = tell(peers_z, [wz.at[z]] * (NZ - 1), wz.at[z], wz_send, wz_recv)
    arrive(0)
    total(0, 0, half, nothing, into(sp4))
    coming_up = [forward(sp4, rp3, 1), None]
    total(0, half, half, nothing, into(sm4, half))
    coming_down = [None, forward(sm4, rm3, -1)]

    def whole(ref):
        return lambda b, span: ref[b, span].astype(jnp.float32)

    def far(ref, lo):
        return lambda b, span: ref[b - lo, span].astype(jnp.float32)

    def step(k, coming, got, out, there, dz):
        arrive(k)
        leaving = [None, None]
        for n in (1, 0) if dz == 1 else (0, 1):
            arrived = nothing
            if coming[n] is not None:
                coming[n].wait_recv()
                arrived = whole(got) if k > 2 else far(got, n * half)
            total(k, n * half, half, arrived, into(out))
            leaving[n] = forward(half_of(out, n), half_of(there, n), dz)
        return leaving

    coming_up = step(1, coming_up, rp3, sp3, rp2, 1)
    coming_down = step(2, coming_down, rm3, sm3, rm2, -1)
    finish(over_z)
    wy[y] = summed(wz, NZ)
    over_y = tell(peers_y, [wy.at[y]] * (NY - 1), wy.at[y], wy_send, wy_recv)
    coming_up = step(3, coming_up, rp2, sp2, rp1, 1)
    coming_down = step(4, coming_down, rm2, sm2, rm1, -1)
    coming_up = step(5, coming_up, rp1, sp1, rp0, 1)
    finish(over_y)
    w_grad[rows_of(f)] = summed(wy, NY) * W_SCALE
    back = tell(
        peers_f, [w_grad.at[rows_of(f)]] * (NF - 1), w_grad.at[rows_of(f)], wg_send, wg_recv
    )
    coming_down = step(6, coming_down, rm1, sm1, rm0, -1)
    arrive(7)

    def local(b, span):
        return local_part[b, span]

    def put_last(b, span, acc):
        h_sum[b, span] = acc

    stores = []
    total(7, 0, BLK, local, put_last)
    for n in range(2):
        coming_up[n].wait_recv()
        coming_down[n].wait_recv()
        for b in range(n * half, n * half + half):
            whole_sum = h_sum[b] + rp0[b].astype(jnp.float32) + rm0[b].astype(jnp.float32)
            h_grad[b] = whole_sum.T.astype(jnp.bfloat16)
        stores.append(
            pltpu.make_async_copy(half_of(h_grad, n), half_of(h_grad_h, n), out_sem.at[n])
        )
        stores[-1].start()
    for copy in hops:
        copy.wait_send()
    for copy in sends.values():
        copy.wait_send()
    finish(back)
    stores.append(pltpu.make_async_copy(w_grad, w_grad_h, out_sem.at[2]))
    stores[-1].start()
    for copy in stores:
        copy.wait()


def scatter(contrib, local_part, w_local, need, peer_need):
    hbm = pl.BlockSpec(memory_space=pl.ANY)
    bf = jnp.bfloat16
    blocks = [BLK // 2] * 2 + [BLK] * 6 + [BLK // 2] * 2 + [BLK] * 6
    return pl.pallas_call(
        scatter_kernel,
        out_shape=(
            VMEM((BLK, TB, TB), bf),
            VMEM((TB, TB), jnp.float32),
        ),
        in_specs=[hbm] * 5,
        out_specs=(pl.BlockSpec(memory_space=VMEM),) * 2,
        scratch_shapes=[
            VMEM((BLK, TB, TB), jnp.float32),
            VMEM((TB, TB), jnp.float32),
            SMEM((1, SLOT, NY * NZ), jnp.int32),
            SMEM((NY - 1, 1, SLOT, NY * NZ), jnp.int32),
            VMEM((BLK, TB, TB), bf),
            VMEM((TB, TB), jnp.float32),
            VMEM((NY - 1, NZ, SLOT, TB, TB), bf),
            VMEM((NZ * SLOT, TB, TB), bf),
        ]
        + [VMEM((n, TB, TB), bf) for n in blocks]
        + [VMEM((BLK, TB, TB), jnp.float32)]
        + [VMEM((n, PIECE, TB), jnp.float32) for n in (NF, NY, NZ)]
        + [DMA, DMA((NY - 1, NZ)), DMA((NY - 1, NZ)), DMA((14,)), DMA((14,))]
        + [DMA((4,)), DMA((3,))]
        + [DMA((n - 1,)) for n in (NF, NF, NY, NY, NZ, NZ, NF, NF)],
        compiler_params=pltpu.CompilerParams(
            collective_id=1, has_side_effects=True, vmem_limit_bytes=56 * 2**20
        ),
    )(contrib, local_part, w_local, need, peer_need)


def body(node_feats, cached_feats, tile_values, tile_row, tile_col, tile_count, need_blocks, weights, grad_out):
    node = node_feats.reshape(BLK, TB, TB)
    cached = cached_feats.reshape(SRC - BLK, TB, TB)
    need = jnp.swapaxes(need_blocks, 1, 2)
    gathered, peer_need = gather(node, cached, need)
    output, contrib, local_part, w_local = layer(
        tile_row, tile_col, tile_count, tile_values, node, cached, gathered, weights,
        grad_out.reshape(BLK, TB, TB),
    )
    h_grad, w_grad = scatter(contrib, local_part, w_local, need, peer_need)
    return output.reshape(BLK * TB, TB), h_grad.reshape(BLK * TB, TB), w_grad


def solution(mesh):
    rows = P(("dom", "feat"), None)
    cubes = P(("dom", "feat"), None, None)
    in_specs = (rows, rows, cubes, rows, rows, P(("dom", "feat")), cubes, P(), rows)
    out_specs = (rows, rows, P())
    return jax.shard_map(body, mesh=mesh, in_specs=in_specs, out_specs=out_specs, check_vma=False)
```

```python
import functools
import math

import jax
import jax.numpy as jnp
from jax import lax
from jax.experimental import pallas as pl
from jax.experimental.pallas import tpu as pltpu
from jax.sharding import PartitionSpec as P

MESH = pl.DeviceIdType.MESH
VMEM = pltpu.VMEM
SMEM = pltpu.SMEM
DMA = pltpu.SemaphoreType.DMA
NY = 4
NZ = 8
TB = 128
SRC = 12
BLK = 8
SLOT = 2
NSLOT = NY * NZ * SLOT
NF = 8
PIECE = TB // NF
W_SCALE = 1.0 / math.sqrt(BLK * TB * NY * NZ * NF)
GROUP = 32
CAST = 8


def _place():
    me = lax.axis_index("dom")
    return me // NZ, lax.rem(me, NZ)


def _at(y, z):
    return {"dom": lax.rem(y + NY, NY) * NZ + lax.rem(z + NZ, NZ)}


def _barrier(loads, peers):
    sem = pltpu.get_barrier_semaphore()
    for peer in peers:
        pl.semaphore_signal(sem, inc=1, device_id=peer, device_id_type=MESH)
    for copy in loads:
        copy.start()
    pl.semaphore_wait(sem, len(peers))


NEAR = (0, -1, 1, -2, 2)
FAR = tuple((2, dy) for dy in (0, 1)) + tuple((-2, dy) for dy in (2, 3))
FAR += tuple((dz, dy) for dy in range(NY) for dz in (1, -1))


def gather_kernel(
    node, cached, need, gathered, peer_need,
    own, need_s, zp0, zm0, zp1, zm1, stage, far_stage, pn_v, pn_s, fn_v, fn_s,
    in_sem, need_send, need_recv, far_send, far_recv, pn_sem, fn_sem, out_sem,
    z_send, z_recv, y_send, y_recv, keep_sem, f_send, f_recv,
):
    y, z = _place()
    loads = [
        pltpu.make_async_copy(node, own.at[pl.ds(0, BLK)], in_sem.at[0]),
        pltpu.make_async_copy(cached, own.at[pl.ds(BLK, SRC - BLK)], in_sem.at[1]),
        pltpu.make_async_copy(need, need_s, in_sem.at[2]),
    ]
    offsets = [(dy, 0) for dy in range(1, NY)]
    offsets += [(dy, dz) for dz in (1, -1) for dy in range(NY)]
    offsets += [(dy, 2) for dy in (0, 1, 2)] + [(dy, -2) for dy in (0, 2, 3)]
    _barrier(loads, [_at(y + dy, z + dz) for dy, dz in offsets])
    for copy in loads[:2]:
        copy.wait()
    half = SRC // 2
    parts = pl.ds(0, half), pl.ds(half, half)

    def chain(stops, slot, dz):
        return [
            [
                pltpu.make_async_remote_copy(
                    src_ref=stops[i].at[part], dst_ref=stops[i + 1].at[part],
                    send_sem=z_send.at[slot + 2 * i + n], recv_sem=z_recv.at[slot + 2 * i + n],
                    device_id=_at(y, z + dz), device_id_type=MESH,
                )
                for n, part in enumerate(parts)
            ]
            for i in range(2)
        ]

    up = chain((own, zp0, zp1), 0, 1)
    down = chain((own, zm0, zm1), 4, -1)
    asks = [
        pltpu.make_async_remote_copy(
            src_ref=need, dst_ref=pn_v.at[dy - 1],
            send_sem=need_send.at[dy - 1], recv_sem=need_recv.at[dy - 1],
            device_id=_at(y + dy, z), device_id_type=MESH,
        )
        for dy in range(1, NY)
    ]
    far_asks = [
        pltpu.make_async_remote_copy(
            src_ref=need, dst_ref=fn_v.at[i], send_sem=far_send.at[i], recv_sem=far_recv.at[i],
            device_id=_at(y - dy, z - dz), device_id_type=MESH,
        )
        for i, (dz, dy) in enumerate(FAR)
    ]
    for copy in asks:
        copy.start()
    for n in range(2):
        up[0][n].start()
        down[0][n].start()
    for copy in far_asks:
        copy.start()
    loads[2].wait()
    for copy in asks:
        copy.wait()
    to_scalar = pltpu.make_async_copy(pn_v, pn_s, pn_sem)
    to_scalar.start()
    to_output = pltpu.make_async_copy(pn_v, peer_need, out_sem)
    to_output.start()
    to_scalar.wait()

    def slots(y0, z0):
        return pl.ds((lax.rem(y0 + NY, NY) * NZ + lax.rem(z0 + NZ, NZ)) * SLOT, SLOT)

    sends = []
    keeps = []

    def serve(buf, k):
        z0 = lax.rem(z + NEAR[k] + NZ, NZ)
        for dy in range(1, NY):
            for s in range(SLOT):
                stage[dy, k, s] = buf[pn_s[NY - 1 - dy, 0, s, y * NZ + z0]]
            copy = pltpu.make_async_remote_copy(
                src_ref=stage.at[dy, k], dst_ref=gathered.at[slots(y, z0)],
                send_sem=y_send.at[dy - 1, k], recv_sem=y_recv.at[dy - 1, k],
                device_id=_at(y + dy, z), device_id_type=MESH,
            )
            copy.start()
            sends.append((dy, k, copy))
        for s in range(SLOT):
            stage[0, k, s] = buf[need_s[0, s, y * NZ + z0]]
        copy = pltpu.make_async_copy(stage.at[0, k], gathered.at[slots(y, z0)], keep_sem.at[k])
        copy.start()
        keeps.append(copy)

    serve(own, 0)
    for n in range(2):
        up[0][n].wait_recv()
        up[1][n].start()
        down[0][n].wait_recv()
        down[1][n].start()
    serve(zp0, 1)
    serve(zm0, 2)
    for copy in far_asks:
        copy.wait()
    to_scalar = pltpu.make_async_copy(fn_v, fn_s, fn_sem)
    to_scalar.start()
    to_scalar.wait()
    for n in range(2):
        up[1][n].wait_recv()
        down[1][n].wait_recv()
    far_sends = []
    for i, (dz, dy) in enumerate(FAR):
        buf, back = (zp1, -2) if dz > 0 else (zm1, 2)
        z0 = lax.rem(z + back + NZ, NZ)
        for s in range(SLOT):
            far_stage[i, s] = buf[fn_s[i, 0, s, y * NZ + z0]]
        copy = pltpu.make_async_remote_copy(
            src_ref=far_stage.at[i], dst_ref=gathered.at[slots(y, z0)],
            send_sem=f_send.at[i], recv_sem=f_recv.at[i],
            device_id=_at(y + dy, z + dz), device_id_type=MESH,
        )
        copy.start()
        far_sends.append(copy)
    serve(zp1, 3)
    serve(zm1, 4)
    for pairs in up + down:
        for copy in pairs:
            copy.wait_send()
    to_output.wait()
    for copy in keeps:
        copy.wait()
    for dy, k, copy in sends:
        copy.wait_send()
        pltpu.make_async_remote_copy(
            src_ref=stage.at[dy, k], dst_ref=gathered.at[slots(y - dy, z + NEAR[k])],
            send_sem=y_send.at[dy - 1, k], recv_sem=y_recv.at[dy - 1, k],
            device_id=_at(y - dy, z), device_id_type=MESH,
        ).wait_recv()
    for i, (dz, dy) in enumerate(FAR):
        far_sends[i].wait_send()
        back = -2 if dz > 0 else 2
        pltpu.make_async_remote_copy(
            src_ref=far_stage.at[i], dst_ref=gathered.at[slots(y - dy, z - dz + back)],
            send_sem=f_send.at[i], recv_sem=f_recv.at[i],
            device_id=_at(y - dy, z - dz), device_id_type=MESH,
        ).wait_recv()


def gather(node, cached, need):
    block = (SRC, TB, TB)
    return pl.pallas_call(
        gather_kernel,
        out_shape=(
            jax.ShapeDtypeStruct((NSLOT, TB, TB), jnp.bfloat16),
            jax.ShapeDtypeStruct((NY - 1, 1, SLOT, NY * NZ), jnp.int32),
        ),
        in_specs=[pl.BlockSpec(memory_space=pl.ANY)] * 3,
        out_specs=(pl.BlockSpec(memory_space=pl.ANY),) * 2,
        scratch_shapes=[
            VMEM(block, jnp.bfloat16),
            SMEM((1, SLOT, NY * NZ), jnp.int32),
            VMEM(block, jnp.bfloat16),
            VMEM(block, jnp.bfloat16),
            VMEM(block, jnp.bfloat16),
            VMEM(block, jnp.bfloat16),
            VMEM((NY, len(NEAR), SLOT, TB, TB), jnp.bfloat16),
            VMEM((len(FAR), SLOT, TB, TB), jnp.bfloat16),
            VMEM((NY - 1, 1, SLOT, NY * NZ), jnp.int32),
            SMEM((NY - 1, 1, SLOT, NY * NZ), jnp.int32),
            VMEM((len(FAR), 1, SLOT, NY * NZ), jnp.int32),
            SMEM((len(FAR), 1, SLOT, NY * NZ), jnp.int32),
            DMA((3,)),
            DMA((NY - 1,)),
            DMA((NY - 1,)),
            DMA((len(FAR),)),
            DMA((len(FAR),)),
            DMA,
            DMA,
            DMA,
            DMA((8,)),
            DMA((8,)),
            DMA((NY - 1, len(NEAR))),
            DMA((NY - 1, len(NEAR))),
            DMA((len(NEAR),)),
            DMA((len(FAR),)),
            DMA((len(FAR),)),
        ],
        compiler_params=pltpu.CompilerParams(
            collective_id=0, has_side_effects=True, vmem_limit_bytes=60 * 2**20
        ),
    )(node, cached, need)


def layer_kernel(
    row_h, col_h, count_h, tiles_h, node, cached, gathered, weights_h, grad_out_h,
    output_h, contrib_h, local_h, w_local_h,
    row, col, count, weights, grad_out, output, contrib, w_local,
    tiles, table, mixed_acc, grads_t, spread, tile_sem, in_sem, out_sem, spread_sem,
):
    index_loads = [
        pltpu.make_async_copy(src, dst, in_sem.at[i])
        for i, (src, dst) in enumerate(((count_h, count), (row_h, row), (col_h, col)))
    ]
    table_loads = [
        pltpu.make_async_copy(gathered, table.at[pl.ds(SRC, NSLOT)], in_sem.at[3]),
        pltpu.make_async_copy(node, table.at[pl.ds(0, BLK)], in_sem.at[4]),
        pltpu.make_async_copy(cached, table.at[pl.ds(BLK, SRC - BLK)], in_sem.at[5]),
    ]
    dense_loads = [
        pltpu.make_async_copy(weights_h, weights, in_sem.at[6]),
        pltpu.make_async_copy(grad_out_h, grad_out, in_sem.at[7]),
    ]
    for copy in index_loads + table_loads:
        copy.start()

    def tile_load(i):
        span = pl.ds(i * GROUP, GROUP)
        return pltpu.make_async_copy(tiles_h.at[span], tiles.at[span], tile_sem.at[i])

    index_loads[0].wait()
    used = count[0]
    groups = (used + GROUP - 1) // GROUP

    def start_tiles(i, _):
        tile_load(i).start()
        return 0

    lax.fori_loop(0, groups, start_tiles, 0)
    for copy in dense_loads:
        copy.start()
    zero_src = SRC + NSLOT
    table[zero_src] = jnp.zeros((TB, TB), jnp.bfloat16)
    grads_t[BLK] = jnp.zeros((TB, TB), jnp.bfloat16)
    mixed_acc[...] = jnp.zeros_like(mixed_acc)

    def clear(c, _):
        spread[c] = jnp.zeros((TB, TB), jnp.float32)
        return 0

    lax.fori_loop(0, SRC + NSLOT, clear, 0)
    for copy in index_loads[1:] + table_loads:
        copy.wait()

    def forward_step(i, _):
        tile_load(i).wait()
        products = []
        for u in range(GROUP):
            t = i * GROUP + u
            c = jnp.where(t < used, col[0, t], zero_src)
            products.append(jnp.dot(tiles[t], table[c], preferred_element_type=jnp.float32))
        for u in range(GROUP):
            r = row[0, i * GROUP + u]
            mixed_acc[r] += products[u]
        return 0

    lax.fori_loop(0, groups, forward_step, 0)
    for copy in dense_loads:
        copy.wait()

    w = weights[...]
    w_sum = jnp.zeros((TB, TB), jnp.float32)
    for r in range(BLK):
        mixed = mixed_acc[r].astype(jnp.bfloat16)
        pre = jnp.dot(mixed, w, preferred_element_type=jnp.float32)
        sig = jax.nn.sigmoid(pre)
        output[r] = (pre * sig).astype(jnp.bfloat16)
        act = (grad_out[r].astype(jnp.float32) * sig * (1.0 + pre * (1.0 - sig))).astype(jnp.bfloat16)
        grads_t[r] = lax.dot_general(
            w, act, (((1,), (1,)), ((), ())), preferred_element_type=jnp.float32
        ).astype(jnp.bfloat16)
        w_sum += lax.dot_general(
            mixed, act, (((0,), (0,)), ((), ())), preferred_element_type=jnp.float32
        )
    w_local[...] = w_sum
    stores = [
        pltpu.make_async_copy(output, output_h, out_sem.at[0]),
        pltpu.make_async_copy(w_local, w_local_h, out_sem.at[1]),
    ]
    for copy in stores:
        copy.start()

    def backward_step(i, _):
        products = []
        for u in range(GROUP):
            t = i * GROUP + u
            r = jnp.where(t < used, row[0, t], BLK)
            products.append(jnp.dot(grads_t[r], tiles[t], preferred_element_type=jnp.float32))
        for u in range(GROUP):
            c = col[0, i * GROUP + u]
            spread[c] += products[u]
        return 0

    lax.fori_loop(0, groups, backward_step, 0)
    stores.append(pltpu.make_async_copy(spread.at[pl.ds(0, BLK)], local_h, out_sem.at[2]))
    stores[-1].start()

    def store_part(i):
        span = pl.ds(i * CAST, CAST)
        return pltpu.make_async_copy(contrib.at[span], contrib_h.at[span], spread_sem.at[i])

    def cast(i, _):
        for u in range(CAST):
            s = i * CAST + u
            contrib[s] = spread[SRC + s].astype(jnp.bfloat16)
        store_part(i).start()
        return 0

    lax.fori_loop(0, NSLOT // CAST, cast, 0)
    for i in range(NSLOT // CAST):
        store_part(i).wait()
    for copy in stores:
        copy.wait()


def layer(row, col, count, tiles, node, cached, gathered, weights, grad_out):
    cap = tiles.shape[0]
    flops = 4 * cap * TB**3
    hbm = pl.BlockSpec(memory_space=pl.ANY)
    bf, f32 = jnp.bfloat16, jnp.float32
    return pl.pallas_call(
        layer_kernel,
        out_shape=(
            jax.ShapeDtypeStruct((BLK, TB, TB), bf),
            jax.ShapeDtypeStruct((NSLOT, TB, TB), bf),
            jax.ShapeDtypeStruct((BLK, TB, TB), f32),
            jax.ShapeDtypeStruct((TB, TB), f32),
        ),
        in_specs=[hbm] * 9,
        out_specs=(hbm,) * 4,
        scratch_shapes=[
            SMEM((1, cap), jnp.int32),
            SMEM((1, cap), jnp.int32),
            SMEM((1,), jnp.int32),
            VMEM((TB, TB), bf),
            VMEM((BLK, TB, TB), bf),
            VMEM((BLK, TB, TB), bf),
            VMEM((NSLOT, TB, TB), bf),
            VMEM((TB, TB), f32),
            VMEM((cap, TB, TB), bf),
            VMEM((SRC + NSLOT + 1, TB, TB), bf),
            VMEM((BLK, TB, TB), f32),
            VMEM((BLK + 1, TB, TB), bf),
            VMEM((SRC + NSLOT, TB, TB), f32),
            DMA((cap // GROUP,)),
            DMA((8,)),
            DMA((3,)),
            DMA((NSLOT // CAST,)),
        ],
        compiler_params=pltpu.CompilerParams(vmem_limit_bytes=60 * 2**20),
        cost_estimate=pl.CostEstimate(
            flops=flops, bytes_accessed=16 * 2**20, transcendentals=BLK * TB * TB
        ),
    )(row, col, count, tiles, node, cached, gathered, weights, grad_out)


SCATTER_ORDER = (4, 3, -3, 2, -2, 1, -1, 0)


def scatter_kernel(
    contrib, local_h, w_local_h, need_h, peer_need_h, h_grad_h, w_grad_h,
    local_part, w_local, need_s, peer_need, h_grad, w_grad, ybuf, ownc, sp4, sm4, sp3, sm3, sp2, sm2, sp1, sm1,
    rp3, rm3, rp2, rm2, rp1, rm1, rp0, rm0, h_sum,
    wf, wy, wz, own_sem, y_send, y_recv, z_send, z_recv,
    load_sem, out_sem, wf_send, wf_recv, wy_send, wy_recv, wz_send, wz_recv, wg_send, wg_recv,
):
    y, z = _place()
    f = lax.axis_index("feat")
    mine = pltpu.make_async_copy(contrib.at[pl.ds(y * NZ * SLOT, NZ * SLOT)], ownc, own_sem)
    loads = [
        pltpu.make_async_copy(src, dst, load_sem.at[i])
        for i, (src, dst) in enumerate(
            (
                (w_local_h, w_local), (local_h, local_part),
                (need_h, need_s), (peer_need_h, peer_need),
            )
        )
    ]
    peers_f = [{"feat": lax.rem(f + df, NF)} for df in range(1, NF)]
    peers_y = [_at(y + dy, z) for dy in range(1, NY)]
    peers_z = [_at(y, z + dz) for dz in range(1, NZ)]
    _barrier([mine] + loads, peers_f + peers_y + peers_z)
    piece = PIECE

    def rows_of(i):
        return pl.ds(pl.multiple_of(i * piece, piece), piece)

    def tell(peers, srcs, dst, send_sem, recv_sem):
        copies = [
            pltpu.make_async_remote_copy(
                src_ref=src, dst_ref=dst, send_sem=send_sem.at[i], recv_sem=recv_sem.at[i],
                device_id=peer, device_id_type=MESH,
            )
            for i, (peer, src) in enumerate(zip(peers, srcs))
        ]
        for copy in copies:
            copy.start()
        return copies

    def finish(copies):
        for copy in copies:
            copy.wait()

    def summed(ref, n):
        acc = ref[0]
        for i in range(1, n):
            acc = acc + ref[i]
        return acc

    loads[0].wait()
    wf[f] = w_local[rows_of(f)]
    over_f = tell(
        peers_f, [w_local.at[rows_of(p["feat"])] for p in peers_f], wf.at[f], wf_send, wf_recv
    )
    sends = {}

    def send(k):
        z0 = lax.rem(z + SCATTER_ORDER[k] + NZ, NZ)
        for dy in range(1, NY):
            theirs = (lax.rem(y + dy, NY) * NZ + z0) * SLOT
            copy = pltpu.make_async_remote_copy(
                src_ref=contrib.at[pl.ds(theirs, SLOT)], dst_ref=ybuf.at[dy - 1, k],
                send_sem=y_send.at[dy - 1, k], recv_sem=y_recv.at[dy - 1, k],
                device_id=_at(y + dy, z), device_id_type=MESH,
            )
            copy.start()
            sends[dy, k] = copy

    for k in range(NZ):
        send(k)
    for copy in [mine] + loads[1:]:
        copy.wait()
    half = BLK // 2
    rows = 32

    def total(k, lo, n, arrived, put):
        z0 = lax.rem(z + SCATTER_ORDER[k] + NZ, NZ)
        ids = [need_s[0, s, y * NZ + z0] for s in range(SLOT)]
        for dy in range(1, NY):
            ids += [peer_need[dy - 1, 0, s, y * NZ + z0] for s in range(SLOT)]

        def part(i, _):
            span = pl.ds(pl.multiple_of(i * rows, rows), rows)
            parts = [ownc[z0 * SLOT + s, span] for s in range(SLOT)]
            for dy in range(1, NY):
                parts += [ybuf[dy - 1, k, s, span] for s in range(SLOT)]
            parts = [p.astype(jnp.float32) for p in parts]
            for b in range(lo, lo + n):
                acc = arrived(b, span)
                for p, which in zip(parts, ids):
                    acc = acc + jnp.where(which == b, p, 0.0)
                put(b, span, acc)
            return 0

        lax.fori_loop(0, TB // rows, part, 0)

    def hop(src, dst, slot, dz):
        return pltpu.make_async_remote_copy(
            src_ref=src, dst_ref=dst, send_sem=z_send.at[slot], recv_sem=z_recv.at[slot],
            device_id=_at(y, z + dz), device_id_type=MESH,
        )

    def nothing(b, span):
        return jnp.zeros((rows, TB), jnp.float32)

    def into(ref, lo=0):
        def put(b, span, acc):
            ref[b - lo, span] = acc.astype(jnp.bfloat16)

        return put

    def arrive(k):
        for dy in range(1, NY):
            sends[dy, k].wait_recv()

    def half_of(ref, n):
        return ref.at[pl.ds(n * half, half)]

    hops = []

    def forward(src, dst, dz):
        hops.append(hop(src, dst, len(hops), dz))
        hops[-1].start()
        return hops[-1]

    finish(over_f)
    wz[z] = summed(wf, NF)
    over_z = tell(peers_z, [wz.at[z]] * (NZ - 1), wz.at[z], wz_send, wz_recv)
    arrive(0)
    total(0, 0, half, nothing, into(sp4))
    coming_up = [forward(sp4, rp3, 1), None]
    total(0, half, half, nothing, into(sm4, half))
    coming_down = [None, forward(sm4, rm3, -1)]

    def whole(ref):
        return lambda b, span: ref[b, span].astype(jnp.float32)

    def far(ref, lo):
        return lambda b, span: ref[b - lo, span].astype(jnp.float32)

    def step(k, coming, got, out, there, dz):
        arrive(k)
        leaving = [None, None]
        for n in (1, 0) if dz == 1 else (0, 1):
            arrived = nothing
            if coming[n] is not None:
                coming[n].wait_recv()
                arrived = whole(got) if k > 2 else far(got, n * half)
            total(k, n * half, half, arrived, into(out))
            leaving[n] = forward(half_of(out, n), half_of(there, n), dz)
        return leaving

    coming_up = step(1, coming_up, rp3, sp3, rp2, 1)
    coming_down = step(2, coming_down, rm3, sm3, rm2, -1)
    finish(over_z)
    wy[y] = summed(wz, NZ)
    over_y = tell(peers_y, [wy.at[y]] * (NY - 1), wy.at[y], wy_send, wy_recv)
    coming_up = step(3, coming_up, rp2, sp2, rp1, 1)
    coming_down = step(4, coming_down, rm2, sm2, rm1, -1)
    coming_up = step(5, coming_up, rp1, sp1, rp0, 1)
    finish(over_y)
    w_grad[rows_of(f)] = summed(wy, NY) * W_SCALE
    back = tell(
        peers_f, [w_grad.at[rows_of(f)]] * (NF - 1), w_grad.at[rows_of(f)], wg_send, wg_recv
    )
    coming_down = step(6, coming_down, rm1, sm1, rm0, -1)
    arrive(7)

    def local(b, span):
        return local_part[b, span]

    def put_last(b, span, acc):
        h_sum[b, span] = acc

    stores = []
    total(7, 0, BLK, local, put_last)
    for n in range(2):
        coming_up[n].wait_recv()
        coming_down[n].wait_recv()
        for b in range(n * half, n * half + half):
            whole_sum = h_sum[b] + rp0[b].astype(jnp.float32) + rm0[b].astype(jnp.float32)
            h_grad[b] = whole_sum.T.astype(jnp.bfloat16)
        stores.append(
            pltpu.make_async_copy(half_of(h_grad, n), half_of(h_grad_h, n), out_sem.at[n])
        )
        stores[-1].start()
    for copy in hops:
        copy.wait_send()
    for copy in sends.values():
        copy.wait_send()
    finish(back)
    stores.append(pltpu.make_async_copy(w_grad, w_grad_h, out_sem.at[2]))
    stores[-1].start()
    for copy in stores:
        copy.wait()


def scatter(contrib, local_part, w_local, need, peer_need):
    hbm = pl.BlockSpec(memory_space=pl.ANY)
    bf = jnp.bfloat16
    blocks = [BLK // 2] * 2 + [BLK] * 6 + [BLK // 2] * 2 + [BLK] * 6
    return pl.pallas_call(
        scatter_kernel,
        out_shape=(
            VMEM((BLK, TB, TB), bf),
            VMEM((TB, TB), jnp.float32),
        ),
        in_specs=[hbm] * 5,
        out_specs=(pl.BlockSpec(memory_space=VMEM),) * 2,
        scratch_shapes=[
            VMEM((BLK, TB, TB), jnp.float32),
            VMEM((TB, TB), jnp.float32),
            SMEM((1, SLOT, NY * NZ), jnp.int32),
            SMEM((NY - 1, 1, SLOT, NY * NZ), jnp.int32),
            VMEM((BLK, TB, TB), bf),
            VMEM((TB, TB), jnp.float32),
            VMEM((NY - 1, NZ, SLOT, TB, TB), bf),
            VMEM((NZ * SLOT, TB, TB), bf),
        ]
        + [VMEM((n, TB, TB), bf) for n in blocks]
        + [VMEM((BLK, TB, TB), jnp.float32)]
        + [VMEM((n, PIECE, TB), jnp.float32) for n in (NF, NY, NZ)]
        + [DMA, DMA((NY - 1, NZ)), DMA((NY - 1, NZ)), DMA((14,)), DMA((14,))]
        + [DMA((4,)), DMA((3,))]
        + [DMA((n - 1,)) for n in (NF, NF, NY, NY, NZ, NZ, NF, NF)],
        compiler_params=pltpu.CompilerParams(
            collective_id=1, has_side_effects=True, vmem_limit_bytes=56 * 2**20
        ),
    )(contrib, local_part, w_local, need, peer_need)


def body(node_feats, cached_feats, tile_values, tile_row, tile_col, tile_count, need_blocks, weights, grad_out):
    node = node_feats.reshape(BLK, TB, TB)
    cached = cached_feats.reshape(SRC - BLK, TB, TB)
    need = jnp.swapaxes(need_blocks, 1, 2)
    gathered, peer_need = gather(node, cached, need)
    output, contrib, local_part, w_local = layer(
        tile_row, tile_col, tile_count, tile_values, node, cached, gathered, weights,
        grad_out.reshape(BLK, TB, TB),
    )
    h_grad, w_grad = scatter(contrib, local_part, w_local, need, peer_need)
    return output.reshape(BLK * TB, TB), h_grad.reshape(BLK * TB, TB), w_grad


def solution(mesh):
    rows = P(("dom", "feat"), None)
    cubes = P(("dom", "feat"), None, None)
    in_specs = (rows, rows, cubes, rows, rows, P(("dom", "feat")), cubes, P(), rows)
    out_specs = (rows, rows, P())
    return jax.shard_map(body, mesh=mesh, in_specs=in_specs, out_specs=out_specs, check_vma=False)
```
